128 devices in a mesh: rows: 16 (over y, z), cols: 8 (over x, core).
Axes of the slice: x: 4, y: 4, z: 4, core: 2. Of those that a mesh axis runs over, the one named last changes fastest.
Arguments:
- iterate: bfloat16 [65536, 128], P(('rows', 'cols')), may hold values from -6 to 6
- blocks: bfloat16 [16, 8, 384, 128, 128], P('rows', 'cols'), may hold values from -0.0546875 to 0.0546875
- block_row: int32 [16, 8, 384], P('rows', 'cols'), may hold values from 0 to 511, as said below
- block_col: int32 [16, 8, 384], P('rows', 'cols'), may hold values from 0 to 511, as said below
- block_count: int32 [16, 8], P('rows', 'cols'), may hold values from 96 to 384, as said below
Outputs:
- search: bfloat16 [65536, 128], P(('rows', 'cols'))
- projected: float32 [256, 256], replicated
The draws below stay inside these ranges and needn't reach their ends.
Inputs may be any that keep to these rules, and one draw needn't show every extreme that they name: block_row[a, b, s] lies in row group a: block rows a * 4 * 8 to (a + 1) * 4 * 8 - 1. block_col[a, b, s] is a block column j with (j // 4) % 8 == b. `block_count`: at least two slots of every device are live; some device has all slots live.
All inputs are finite; a program needn't handle non-finite values.
Results may differ from the reference program's by a relative error of at most 0.0019.
Values may be sent and summed in bfloat16 or wider, within the bound.
A program may use at most 192 MiB of HBM per device.

```python
import jax
import jax.numpy as jnp
from jax import lax

BS = 128
K = 128
BR_DEV = 4
NNZ_DEV = 384
N = 65536
N_ROWS = 16
N_COLS = 8


def draw_block_row(key, part):
    key = jax.random.fold_in(key, 11)
    group_blocks = BR_DEV * N_COLS
    row_local = jax.random.randint(key, (N_ROWS, N_COLS, NNZ_DEV), 0, group_blocks)
    slot_ids = jnp.arange(NNZ_DEV)[None, None, :]
    row_local = jnp.where(slot_ids == 0, 0, jnp.where(slot_ids == 1, group_blocks - 1, row_local))
    row_base = (jnp.arange(N_ROWS) * group_blocks)[:, None, None]
    return (row_local + row_base).astype(jnp.int32)


def draw_block_col(key, part):
    key = jax.random.fold_in(key, 12)
    key_one, key_two = jax.random.split(key)
    row_owner = jax.random.randint(key_one, (N_ROWS, N_COLS, NNZ_DEV), 0, N_ROWS)
    within = jax.random.randint(key_two, (N_ROWS, N_COLS, NNZ_DEV), 0, BR_DEV)
    slot_ids = jnp.arange(NNZ_DEV)[None, None, :]
    row_owner = jnp.where(slot_ids == 0, 0, jnp.where(slot_ids == 1, N_ROWS - 1, row_owner))
    within = jnp.where(slot_ids == 0, 0, jnp.where(slot_ids == 1, BR_DEV - 1, within))
    col_dev = jnp.arange(N_COLS)[None, :, None]
    return ((row_owner * N_COLS + col_dev) * BR_DEV + within).astype(jnp.int32)


def draw_block_count(key, part):
    key = jax.random.fold_in(key, 13)
    key_one, key_two = jax.random.split(key)
    counts = jax.random.randint(key_one, (N_ROWS, N_COLS), NNZ_DEV // 4, NNZ_DEV + 1)
    chosen = jax.random.randint(key_two, (), 0, N_ROWS * N_COLS)
    flat_ids = jnp.arange(N_ROWS * N_COLS).reshape(N_ROWS, N_COLS)
    return jnp.where(flat_ids == chosen, NNZ_DEV, counts).astype(jnp.int32)


def shard_levels(stream_key, shape, pieces, least, top_value):
    factor_of = 1.0
    for axis_at, blocks in pieces:
        steps = jax.random.uniform(jax.random.fold_in(jax.random.fold_in(stream_key, 6), axis_at), (blocks,), jnp.float32, least / len(pieces), top_value / len(pieces))
        factor_of = factor_of * jnp.repeat(jnp.exp(steps), shape[axis_at] // blocks).reshape((-1,) + (1,) * (len(shape) - 1 - axis_at))
    return factor_of


def centred(key, shape, deviation, limit, cuts=(), held_as=jnp.bfloat16):
    gain = shard_levels(key, shape, cuts, -0.22, 0.18) if cuts else 1.0
    result = jax.random.normal(key, shape, jnp.float32) * deviation * gain
    return jnp.minimum(jnp.maximum(result, -limit), limit).astype(held_as)


def setup_inputs(seed: int = 0) -> dict:
    key_list = jax.random.split(jax.random.key(seed), 6)
    return {
        "iterate": centred(key_list[0], (N, K), 1.0, 6.0, ((0, 128),)),
        "blocks": centred(key_list[1], (N_ROWS, N_COLS, NNZ_DEV, BS, BS), (BS * NNZ_DEV // BR_DEV) ** -0.5, 0.0546875, ((0, 16), (1, 8))),
        "block_row": draw_block_row(jax.random.fold_in(key_list[5], 71), 0),
        "block_col": draw_block_col(jax.random.fold_in(key_list[5], 71), 0),
        "block_count": draw_block_count(jax.random.fold_in(key_list[5], 71), 0),
    }


def inner(left, right):
    return jnp.einsum('ik,il->kl', left, right, precision=lax.Precision.HIGHEST)

def reference(iterate, blocks, block_row, block_col, block_count):
    row_groups, col_groups, slot_count = block_row.shape
    node_total = iterate.shape[0]
    block_total = node_total // BS
    group_blocks = block_total // row_groups
    inverse = 1.0 / node_total

    def apply_graph(field):
        tile_set = field.reshape(block_total, BS, K)

        def one_device(running, flat_index):
            row_dev = flat_index // col_groups
            col_dev = flat_index % col_groups
            values = blocks[row_dev, col_dev]
            row_local = block_row[row_dev, col_dev] - row_dev * group_blocks
            col_global = block_col[row_dev, col_dev]
            live_mask = jnp.arange(slot_count) < block_count[row_dev, col_dev]
            row_hot = ((row_local[None, :] == jnp.arange(group_blocks)[:, None]) & live_mask[None, :]).astype(jnp.float32)
            picked = tile_set[col_global].astype(jnp.float32)
            product = jnp.einsum('nab,nbk->nak', values.astype(jnp.float32), picked, precision=lax.Precision.HIGHEST)
            summed = jnp.einsum('gn,nak->gak', row_hot, product, precision=lax.Precision.HIGHEST)
            row_weight = jnp.einsum('gn,na->ga', row_hot, jnp.sum(values.astype(jnp.float32), axis=2), precision=lax.Precision.HIGHEST)
            adj_all, deg_all = running
            adj_all = adj_all.at[row_dev].add(summed.reshape(group_blocks * BS, K))
            deg_all = deg_all.at[row_dev].add(row_weight.reshape(group_blocks * BS))
            return ((adj_all, deg_all), None)
        start = (jnp.zeros((row_groups, group_blocks * BS, K), jnp.float32), jnp.zeros((row_groups, group_blocks * BS), jnp.float32))
        (adj_all, deg_all), unused = lax.scan(one_device, start, jnp.arange(row_groups * col_groups, dtype=jnp.int32))
        return (adj_all.reshape(node_total, K), deg_all.reshape(node_total))
    adj_x, degree = apply_graph(iterate)
    iter_f = iterate.astype(jnp.float32)
    lap_x = degree[:, None] * iter_f - adj_x
    theta_mat = inverse * inner(iter_f, lap_x)
    residual = lap_x - jnp.dot(iter_f, theta_mat, precision=lax.Precision.HIGHEST)
    correlation = inverse * inner(iter_f, residual)
    cleaned = residual - jnp.dot(iter_f, correlation, precision=lax.Precision.HIGHEST)
    gram_mat = inverse * inner(cleaned, cleaned)
    lower_factor = jnp.linalg.cholesky(gram_mat)
    search = lax.linalg.triangular_solve(lower_factor, cleaned, left_side=False, lower=True, transpose_a=True).astype(jnp.bfloat16)
    adj_q, unused_degree = apply_graph(search)
    search_f = search.astype(jnp.float32)
    lap_q = degree[:, None] * search_f - adj_q
    cross_xq = inverse * inner(iter_f, lap_q)
    cross_qx = inverse * inner(search_f, lap_x)
    inner_qq = inverse * inner(search_f, lap_q)
    top_half = jnp.concatenate([theta_mat, cross_xq], axis=1)
    bottom_half = jnp.concatenate([cross_qx, inner_qq], axis=1)
    return (search, jnp.concatenate([top_half, bottom_half], axis=0))
```

```python
import jax
import jax.numpy as jnp
from jax import lax
from jax.experimental import pallas as pl
from jax.experimental.pallas import tpu as pltpu
from jax.sharding import PartitionSpec as P

BS = 128
NY = 4
NZ = 4
NX = 4
NCOL = 8
GROUP = 32
SLOTS = 384
PAIRS = (SLOTS + GROUP) // 2
UNROLL = 16
DEG = 8
N_SEM = 112

F32 = jnp.float32
BF16 = jnp.bfloat16
HI = lax.Precision.HIGHEST


def nt(a, b, precision=None):
    return lax.dot_general(a, b, (((1,), (1,)), ((), ())), precision=precision, preferred_element_type=F32)


def nn(a, b, precision=None):
    return jnp.dot(a, b, precision=precision, preferred_element_type=F32)


def iota(shape, dim):
    return lax.broadcasted_iota(jnp.int32, shape, dim)


def flag(mask):
    return jnp.where(mask, 1.0, 0.0).astype(F32)


def sort_slots(row, col, count, a):
    live = iota((1, SLOTS), 1) < count
    local = jnp.where(live, row - a * GROUP, 2 * GROUP - 1)
    owner = col >> 5
    part = col & 3
    oy, oz = owner >> 2, owner & 3
    piece = part >> 1
    place = jnp.where(piece == 0, oz * 4 + oy, oy * 4 + oz)
    tile = piece * 32 + place * 2 + (part & 1)
    local_f = local.astype(F32)
    row_t = jnp.broadcast_to(local_f, (BS, SLOTS)).T
    lane = iota((SLOTS, BS), 1).astype(F32)
    hits = flag(row_t == lane)
    counts = jnp.sum(hits, axis=0, keepdims=True)
    counts = jnp.where(iota((1, BS), 1) < GROUP, counts, 0.0)
    pairs = ((counts.astype(jnp.int32) + 1) >> 1).astype(F32)
    upper = flag(iota((BS, BS), 0) < iota((BS, BS), 1)).astype(BF16)
    start = nn(jnp.broadcast_to(pairs, (16, BS)).astype(BF16), upper)[:1]
    row_w = jnp.concatenate([row_t] * (SLOTS // BS), axis=1)
    before = (row_w == local_f) & (iota((SLOTS, SLOTS), 1) < iota((SLOTS, SLOTS), 0))
    within = jnp.sum(flag(before), axis=1, keepdims=True)
    base = jnp.sum(hits * start, axis=1, keepdims=True)
    pos = 2.0 * base + within
    pos = jnp.where(row_t[:, :1] < GROUP, pos, 4096.0)
    onehot = flag(pos == iota((SLOTS, 512), 1).astype(F32)).astype(BF16)
    slot = iota((1, SLOTS), 1)
    values = jnp.concatenate(
        [(slot >> 4).astype(F32), (slot & 15).astype(F32), tile.astype(F32), jnp.ones((1, SLOTS), F32),
         jnp.zeros((12, SLOTS), F32)], axis=0).astype(BF16)
    placed = nn(values, onehot)
    perm = placed[0:1] * 16.0 + placed[1:2] + SLOTS * (1.0 - placed[3:4])
    start_t = jnp.broadcast_to(start, (BS, BS)).T
    pairs_t = jnp.broadcast_to(pairs, (BS, BS)).T
    lane4 = iota((BS, 512), 1).astype(F32)
    first = jnp.sum(flag((start_t[:, :1] == lane4) & (pairs_t[:, :1] > 0.0)), axis=0, keepdims=True)
    pad = jnp.zeros((1, 512 - BS), F32)
    last = jnp.concatenate([jnp.maximum(start + pairs - 1.0, 0.0), pad], axis=1)
    filled = jnp.concatenate([jnp.minimum(pairs, 1.0), pad], axis=1)
    ints = jnp.concatenate([perm, placed[2:3], last, jnp.zeros((5, 512), F32)], axis=0).astype(jnp.int32)
    floats = jnp.concatenate([1.0 - first, filled, jnp.zeros((6, 512), F32)], axis=0)
    return ints, floats


def apply_kernel(x_ref, w_hbm, row_ref, col_ref, cnt_ref, lap_ref, amat_ref, bmat_ref,
                 w_ref, slab1, slab2, prod, xt_ref, ints_v, floats_v, ints_s, floats_s,
                 sib1_s, sib1_r, sib2_s, sib2_r, hi_s, hi_r, lo_s, lo_r, deg_s, deg_r, q_s, q_r,
                 own1, own2, deg_ref,
                 a_part, a_r1, a_b2, a_b3, b_part, b_r1, b_b2, b_b3,
                 send_sem, recv_sem, local_sem):
    a = lax.axis_index("rows")
    b = lax.axis_index("cols")
    y, z = a // NZ, a % NZ
    xx, core = b // 2, b % 2
    counter = [0]

    def ydev(d):
        return {"rows": ((y + d + NY) % NY) * NZ + z, "cols": b}

    def zdev(d):
        return {"rows": y * NZ + (z + d + NZ) % NZ, "cols": b}

    def coldev(d):
        return {"rows": a, "cols": (b + d) % NCOL}

    def xdev(d):
        return {"rows": a, "cols": ((xx + d) % NX) * 2 + core}

    sibling = {"rows": a, "cols": xx * 2 + (1 - core)}
    sent = []

    def send(src, dst, device):
        k = counter[0]
        counter[0] += 1
        copy = pltpu.make_async_remote_copy(
            src_ref=src, dst_ref=dst, send_sem=send_sem.at[k], recv_sem=recv_sem.at[k],
            device_id=device, device_id_type=pl.DeviceIdType.MESH)
        copy.start()
        sent.append(copy)
        return copy

    w_copy = pltpu.make_async_copy(w_hbm, w_ref.at[pl.ds(0, SLOTS)], local_sem.at[0])
    w_copy.start()

    barrier = pltpu.get_barrier_semaphore()
    partners = [coldev(d) for d in range(1, NCOL)] + [ydev(d) for d in (1, 2, 3)] + [zdev(d) for d in (1, 2, 3)]
    for device in partners:
        pl.semaphore_signal(barrier, inc=1, device_id=device, device_id_type=pl.DeviceIdType.MESH)

    place = ((z, y), (y, z))

    def span(p, i, j, size):
        return pl.ds(p * 32 + (i * 4 + j) * 2, size)

    for r in range(4):
        xt = x_ref[r * BS:(r + 1) * BS, :].astype(F32).T
        xt_ref[r] = xt
        p, t = r // 2, r % 2
        slab1[p * 32 + (place[p][0] * 4 + place[p][1]) * 2 + t] = xt.astype(BF16)

    pl.semaphore_wait(barrier, len(partners))

    def gather(slab):
        def first(p, d):
            return ydev(d) if p == 0 else zdev(d)

        def second(p, d):
            return zdev(d) if p == 0 else ydev(d)

        near = []
        for p in range(2):
            i, j = place[p]
            own = slab.at[span(p, i, j, 2)]
            near.append((send(own, own, first(p, 1)), send(own, own, first(p, -1))))
        yield
        far = []
        for p in range(2):
            i, j = place[p]
            near[p][0].wait_recv()
            one = slab.at[span(p, i, (j + 3) % 4, 1)]
            fwd_r = send(one, one, first(p, 1))
            near[p][1].wait_recv()
            two = slab.at[pl.ds(p * 32 + (i * 4 + (j + 1) % 4) * 2 + 1, 1)]
            fwd_l = send(two, two, first(p, -1))
            far.append((fwd_r, fwd_l))
        yield
        wide = []
        for p in range(2):
            i, j = place[p]
            far[p][0].wait_recv()
            far[p][1].wait_recv()
            low = slab.at[span(p, i, 0, 4)]
            high = slab.at[span(p, i, 2, 4)]
            low_r = send(low, low, second(p, 1))
            high_l = send(high, high, second(p, -1))
            high_r = send(high, high, second(p, 1))
            low_l = send(low, low, second(p, -1))
            wide.append((low_r, high_l, high_r, low_l))
        yield
        rest = []
        for p in range(2):
            i, j = place[p]
            wide[p][0].wait_recv()
            low = slab.at[span(p, (i + 3) % 4, 0, 4)]
            rest.append(send(low, low, second(p, 1)))
            wide[p][1].wait_recv()
            high = slab.at[span(p, (i + 1) % 4, 2, 4)]
            rest.append(send(high, high, second(p, -1)))
        yield
        for p in range(2):
            wide[p][2].wait_recv()
            wide[p][3].wait_recv()
        for copy in rest:
            copy.wait_recv()
        yield

    g1 = gather(slab1)
    next(g1)
    w_ref[SLOTS] = jnp.zeros((BS, BS), BF16)
    ints, floats = sort_slots(row_ref[...], col_ref[...], cnt_ref[0, 0], a)
    ints_v[...] = ints
    floats_v[...] = floats
    ints_copy = pltpu.make_async_copy(ints_v, ints_s, local_sem.at[1])
    floats_copy = pltpu.make_async_copy(floats_v, floats_s, local_sem.at[2])
    ints_copy.start()
    floats_copy.start()
    next(g1)
    next(g1)
    ints_copy.wait()
    floats_copy.wait()
    next(g1)
    xx_mat = sum(nt(xt_ref[r].astype(BF16), xt_ref[r].astype(BF16)) for r in range(4))
    a_part[:, 0] = xx_mat.reshape(8, 16, BS)
    w_copy.wait()
    next(g1)

    def pick(kind, at, top):
        return jnp.clip(ints_s[kind, at], 0, top)

    def product(slab, with_degree):
        rows = BS + DEG if with_degree else BS
        ones = jnp.ones((16, 2 * BS), BF16)

        def body(n, acc):
            for u in range(UNROLL):
                s = n * UNROLL + u
                left = jnp.concatenate([slab[pick(1, 2 * s, 63)], slab[pick(1, 2 * s + 1, 63)]], axis=1)
                if with_degree:
                    left = jnp.concatenate([left, ones], axis=0)
                right = jnp.concatenate([w_ref[pick(0, 2 * s, SLOTS)], w_ref[pick(0, 2 * s + 1, SLOTS)]], axis=1)
                acc = acc * floats_s[0, s] + nt(left, right)[:rows]
                prod[s, :rows] = acc
            return acc

        lax.fori_loop(0, PAIRS // UNROLL, body, jnp.zeros((rows, BS), F32))

    def tile(g, rows):
        return prod[pick(2, g, PAIRS - 1), :rows] * floats_s[1, g]

    def order(d):
        return (xx + d) % NX

    product(slab1, True)
    rows = BS + DEG
    from_sib = {}
    for d in (2, 1, 3, 0):
        for r in range(4):
            sib1_s[d, r] = tile((order(d) * 2 + (1 - core)) * 4 + r, rows)
        from_sib[d] = send(sib1_s.at[d], sib1_r.at[d], sibling)
    hi_copy, deg_copy = {}, {}
    for d in (2, 1, 3, 0):
        from_sib[d].wait_recv()
        for r in range(4):
            total = tile((order(d) * 2 + core) * 4 + r, rows) + sib1_r[d, r]
            if d:
                high = total[:BS].astype(BF16)
                hi_s[d - 1, r] = high
                lo_s[d - 1, r] = (total[:BS] - high.astype(F32)).astype(BF16)
                deg_s[d - 1, r] = total[BS:]
            else:
                own1[r] = total[:BS]
                deg_ref[r] = total[BS:]
        if d:
            deg_copy[d] = send(deg_s.at[d - 1], deg_r.at[d - 1], xdev(d))
            hi_copy[d] = send(hi_s.at[d - 1], hi_r.at[d - 1], xdev(d))
    for d in (1, 3, 2):
        deg_copy[d].wait_recv()
        hi_copy[d].wait_recv()
    for r in range(4):
        degree = deg_ref[r] + deg_r[0, r] + deg_r[1, r] + deg_r[2, r]
        deg_ref[r] = degree
        spread = jnp.broadcast_to(degree[:1], (BS, BS))
        summed = own1[r] + hi_r[0, r].astype(F32) + hi_r[1, r].astype(F32) + hi_r[2, r].astype(F32)
        lap = spread * xt_ref[r] - summed
        own1[r] = lap
        p, t = r // 2, r % 2
        slab2[p * 32 + (place[p][0] * 4 + place[p][1]) * 2 + t] = lap.astype(BF16)
    g2 = gather(slab2)
    next(g2)
    lo_copy = {d: send(lo_s.at[d - 1], lo_r.at[d - 1], xdev(d)) for d in (2, 1, 3)}
    next(g2)
    next(g2)
    for d in (1, 3, 2):
        lo_copy[d].wait_recv()
    for r in range(4):
        lap_ref[r] = own1[r] - (lo_r[0, r].astype(F32) + lo_r[1, r].astype(F32) + lo_r[2, r].astype(F32))

    def joined(ref):
        return jnp.concatenate([ref[r] for r in range(4)], axis=1)

    def all_reduce(part, r1, b2, b3, res):
        copies = [send(part.at[(b + d) % NCOL], r1.at[d - 1], coldev(d)) for d in range(1, NCOL)]
        yield
        for copy in copies:
            copy.wait_recv()
        total = part[b]
        for d in range(1, NCOL):
            total = total + r1[d - 1]
        b2[y] = total
        copies = [send(b2.at[y], b2.at[y], ydev(d)) for d in (1, 2, 3)]
        yield
        for copy in copies:
            copy.wait_recv()
        b3[z] = b2[0] + b2[1] + b2[2] + b2[3]
        copies = [send(b3.at[z], b3.at[z], zdev(d)) for d in (1, 2, 3)]
        yield
        for copy in copies:
            copy.wait_recv()
        res[b] = b3[0] + b3[1] + b3[2] + b3[3]
        copies = [send(res.at[b], res.at[b], coldev(d)) for d in range(1, NCOL)]
        yield
        for copy in copies:
            copy.wait_recv()
        yield

    lap_all = joined(lap_ref)
    a_part[:, 1] = nt(joined(xt_ref), lap_all, HI).reshape(8, 16, BS)
    a_part[:, 2] = nt(lap_all, lap_all, HI).reshape(8, 16, BS)
    next(g2)
    reduce_a = all_reduce(a_part, a_r1, a_b2, a_b3, amat_ref)
    next(reduce_a)
    next(reduce_a)
    next(g2)
    next(reduce_a)

    product(slab2, False)
    from_sib = {}
    for d in (2, 1, 3, 0):
        for r in range(4):
            sib2_s[d, r] = tile((order(d) * 2 + (1 - core)) * 4 + r, BS).astype(BF16)
        from_sib[d] = send(sib2_s.at[d], sib2_r.at[d], sibling)
    q_copy = {}
    for d in (2, 1, 3, 0):
        from_sib[d].wait_recv()
        for r in range(4):
            total = tile((order(d) * 2 + core) * 4 + r, BS) + sib2_r[d, r].astype(F32)
            if d:
                q_s[d - 1, r] = total.astype(BF16)
            else:
                own2[r] = total
        if d:
            q_copy[d] = send(q_s.at[d - 1], q_r.at[d - 1], xdev(d))
    next(reduce_a)
    for d in (1, 3, 2):
        q_copy[d].wait_recv()
    for r in range(4):
        spread = jnp.broadcast_to(deg_ref[r][:1], (BS, BS))
        summed = own2[r] + q_r[0, r].astype(F32) + q_r[1, r].astype(F32) + q_r[2, r].astype(F32)
        own2[r] = spread * lap_ref[r] - summed
    y_all = joined(own2)
    b_part[:, 0] = nt(joined(xt_ref), y_all, HI).reshape(8, 16, BS)
    b_part[:, 1] = nt(joined(lap_ref), y_all, HI).reshape(8, 16, BS)
    reduce_b = all_reduce(b_part, b_r1, b_b2, b_b3, bmat_ref)
    next(reduce_b)
    next(reduce_a)
    for unused in range(4):
        next(reduce_b)
    for copy in sent:
        copy.wait_send()


def factor_inverse(gram):
    left = [gram[8 * i:8 * i + 8] for i in range(16)]
    right = [flag(iota((8, BS), 1) == iota((8, BS), 0) + 8 * i) for i in range(16)]
    sub = iota((8, 1), 0)
    out = []
    for k in range(16):
        scale = jnp.zeros((8, 1), F32)
        for j in range(8):
            c = 8 * k + j
            root = lax.rsqrt(left[k][j:j + 1, c:c + 1])
            inv = root * root
            scale = jnp.where(sub == j, root, scale)
            lrow = left[k][j:j + 1] * inv
            rrow = right[k][j:j + 1] * inv
            for i in range(k, 16):
                f = left[i][:, c:c + 1]
                if i == k:
                    f = jnp.where(sub > j, f, 0.0)
                left[i] = left[i] - f * lrow
                right[i] = right[i] - f * rrow
        out.append(right[k] * scale)
    return jnp.concatenate(out, axis=0)


def finish_kernel(inverse, x_ref, lap_ref, amat_ref, bmat_ref, search_ref, proj_ref):
    def mat(ref, m):
        return ref[:, m].reshape(BS, BS) * inverse

    g, theta, s = mat(amat_ref, 0), mat(amat_ref, 1), mat(amat_ref, 2)
    m = 2.0 * theta - nn(g, theta, HI)
    m_t = m.T
    cross = nn(m_t, theta, HI)
    gram = s - cross.T - cross + nn(m_t, nn(g, m, HI), HI)
    t_t = factor_inverse(gram)
    mt_t = nt(t_t, m, HI)
    x_f = x_ref[...].astype(F32)
    for r in range(4):
        part = nn(t_t, lap_ref[r], HI) - nt(mt_t, x_f[r * BS:(r + 1) * BS], HI)
        search_ref[r * BS:(r + 1) * BS, :] = part.T.astype(BF16)
    q1 = mat(bmat_ref, 0) - nn(theta, m, HI)
    q2 = mat(bmat_ref, 1) - nn(s, m, HI) - nn(m_t, q1, HI)
    proj_ref[:BS, :BS] = theta
    proj_ref[:BS, BS:] = nt(q1, t_t, HI)
    proj_ref[BS:, :BS] = nn(t_t, s - cross, HI)
    proj_ref[BS:, BS:] = nt(nn(t_t, q2, HI), t_t, HI)


def shards(iterate, blocks, block_row, block_col, block_count):
    vmem = pl.BlockSpec(memory_space=pltpu.VMEM)
    shape = jax.ShapeDtypeStruct
    rows1 = BS + DEG

    def sds(*dims, dtype=F32):
        return pltpu.VMEM(dims, dtype)

    lap, amat, bmat = pl.pallas_call(
        apply_kernel,
        out_shape=(shape((4, BS, BS), F32), shape((8, 3, 16, BS), F32), shape((8, 2, 16, BS), F32)),
        in_specs=[vmem, pl.BlockSpec(memory_space=pl.ANY), vmem, vmem,
                  pl.BlockSpec(memory_space=pltpu.SMEM)],
        out_specs=(vmem, vmem, vmem),
        scratch_shapes=[
            sds(SLOTS + 1, BS, BS, dtype=BF16), sds(64, BS, BS, dtype=BF16), sds(64, BS, BS, dtype=BF16),
            sds(PAIRS, rows1, BS), sds(4, BS, BS), sds(8, 512, dtype=jnp.int32), sds(8, 512),
            pltpu.SMEM((8, 512), jnp.int32), pltpu.SMEM((8, 512), F32),
            sds(4, 4, rows1, BS), sds(4, 4, rows1, BS),
            sds(4, 4, BS, BS, dtype=BF16), sds(4, 4, BS, BS, dtype=BF16),
            sds(3, 4, BS, BS, dtype=BF16), sds(3, 4, BS, BS, dtype=BF16),
            sds(3, 4, BS, BS, dtype=BF16), sds(3, 4, BS, BS, dtype=BF16),
            sds(3, 4, DEG, BS), sds(3, 4, DEG, BS),
            sds(3, 4, BS, BS, dtype=BF16), sds(3, 4, BS, BS, dtype=BF16),
            sds(4, BS, BS), sds(4, BS, BS), sds(4, DEG, BS),
            sds(8, 3, 16, BS), sds(7, 3, 16, BS), sds(4, 3, 16, BS), sds(4, 3, 16, BS),
            sds(8, 2, 16, BS), sds(7, 2, 16, BS), sds(4, 2, 16, BS), sds(4, 2, 16, BS),
            pltpu.SemaphoreType.DMA((N_SEM,)), pltpu.SemaphoreType.DMA((N_SEM,)), pltpu.SemaphoreType.DMA((3,)),
        ],
        compiler_params=pltpu.CompilerParams(
            collective_id=0, has_side_effects=True, vmem_limit_bytes=60 * 1024 * 1024),
        name="apply_twice",
    )(iterate, blocks.reshape(SLOTS, BS, BS), block_row.reshape(1, SLOTS), block_col.reshape(1, SLOTS),
      block_count.reshape(1, 1))
    node_total = iterate.shape[0] * lax.axis_size("rows") * lax.axis_size("cols")

    def finish(*refs):
        finish_kernel(1.0 / node_total, *refs)

    return pl.pallas_call(
        finish,
        out_shape=(shape(iterate.shape, BF16), shape((2 * BS, 2 * BS), F32)),
        in_specs=[vmem] * 4,
        out_specs=(vmem, vmem),
        compiler_params=pltpu.CompilerParams(vmem_limit_bytes=32 * 1024 * 1024),
        name="finish",
    )(iterate, lap, amat, bmat)


def solution(mesh):
    placed = (
        P(("rows", "cols"), None),
        P("rows", "cols", None, None, None),
        P("rows", "cols", None),
        P("rows", "cols", None),
        P("rows", "cols"),
    )
    return jax.shard_map(
        shards,
        mesh=mesh,
        in_specs=placed,
        out_specs=(P(("rows", "cols"), None), P()),
        check_vma=False,
    )
```

```python
import math

import jax
import jax.numpy as jnp
from jax import lax
from jax.experimental import pallas as pl
from jax.experimental.pallas import tpu as pltpu
from jax.sharding import PartitionSpec as P

BS = 128
NY = 4
NZ = 4
NX = 4
NCOL = 8
GROUP = 32
SLOTS = 384
PAIRS = (SLOTS + GROUP) // 2
UNROLL = 52
PART = 96
DEG = 8
N_SEM = 120
HALF = BS // 2
BLOCK_BYTES = BS * BS * 2

F32 = jnp.float32
BF16 = jnp.bfloat16
HI = lax.Precision.HIGHEST


def nt(a, b, precision=None):
    return lax.dot_general(a, b, (((1,), (1,)), ((), ())), precision=precision, preferred_element_type=F32)


def nn(a, b, precision=None):
    return jnp.dot(a, b, precision=precision, preferred_element_type=F32)


def iota(shape, dim):
    return lax.broadcasted_iota(jnp.int32, shape, dim)


def flag(mask):
    return jnp.where(mask, 1.0, 0.0).astype(F32)


def sort_slots(row, col, count, a):
    live = iota((1, SLOTS), 1) < count
    local = jnp.where(live, row - a * GROUP, 2 * GROUP - 1)
    owner = col >> 5
    part = col & 3
    oy, oz = owner >> 2, owner & 3
    piece = part >> 1
    place = jnp.where(piece == 0, oz * 4 + oy, oy * 4 + oz)
    tile = piece * 32 + place * 2 + (part & 1)
    local_f = local.astype(F32)
    row_t = jnp.broadcast_to(local_f, (BS, SLOTS)).T
    lane = iota((SLOTS, BS), 1).astype(F32)
    hits = flag(row_t == lane)
    counts = jnp.sum(hits, axis=0, keepdims=True)
    counts = jnp.where(iota((1, BS), 1) < GROUP, counts, 0.0)
    pairs = ((counts.astype(jnp.int32) + 1) >> 1).astype(F32)
    upper = flag(iota((BS, BS), 0) < iota((BS, BS), 1)).astype(BF16)
    start = nn(jnp.broadcast_to(pairs, (16, BS)).astype(BF16), upper)[:1]
    row_w = jnp.concatenate([row_t] * (SLOTS // BS), axis=1)
    before = (row_w == local_f) & (iota((SLOTS, SLOTS), 1) < iota((SLOTS, SLOTS), 0))
    within = jnp.sum(flag(before), axis=1, keepdims=True)
    base = jnp.sum(hits * start, axis=1, keepdims=True)
    pos = 2.0 * base + within
    pos = jnp.where(row_t[:, :1] < GROUP, pos, 4096.0)
    onehot = flag(pos == iota((SLOTS, 512), 1).astype(F32)).astype(BF16)
    slot = iota((1, SLOTS), 1)
    values = jnp.concatenate(
        [(slot >> 4).astype(F32), (slot & 15).astype(F32), tile.astype(F32), jnp.ones((1, SLOTS), F32),
         jnp.zeros((12, SLOTS), F32)], axis=0).astype(BF16)
    placed = nn(values, onehot)
    perm = placed[0:1] * 16.0 + placed[1:2] + SLOTS * (1.0 - placed[3:4])
    start_t = jnp.broadcast_to(start, (BS, BS)).T
    pairs_t = jnp.broadcast_to(pairs, (BS, BS)).T
    lane4 = iota((BS, 512), 1).astype(F32)
    first = jnp.sum(flag((start_t[:, :1] == lane4) & (pairs_t[:, :1] > 0.0)), axis=0, keepdims=True)
    pad = jnp.zeros((1, 512 - BS), F32)
    last = jnp.concatenate([jnp.maximum(start + pairs - 1.0, 0.0), pad], axis=1)
    filled = jnp.concatenate([jnp.minimum(pairs, 1.0), pad], axis=1)
    ints = jnp.concatenate([perm, placed[2:3], last, jnp.zeros((5, 512), F32)], axis=0).astype(jnp.int32)
    floats = jnp.concatenate([1.0 - first, filled, jnp.zeros((6, 512), F32)], axis=0)
    return ints, floats


def factor_inverse(gram):
    left = [gram[8 * i:8 * i + 8] for i in range(16)]
    right = [flag(iota((8, BS), 1) == iota((8, BS), 0) + 8 * i) for i in range(16)]
    sub = iota((8, BS), 0)
    out = []

    def wide(v):
        return jnp.broadcast_to(v, (8, BS))

    for k in range(16):
        c = 8 * k
        lanes = [wide(left[k][:, c + n:c + n + 1]) for n in range(8)]
        elem = [[wide(lanes[n][j:j + 1]) if n <= j else None for n in range(8)] for j in range(8)]
        inv = [[None] * 8 for unused in range(8)]
        roots, pivots = [], []
        for j in range(8):
            root = lax.rsqrt(elem[j][j])
            roots.append(root)
            pivot = root * root
            pivots.append(pivot)
            mult = [elem[i][j] * pivot if i > j else None for i in range(8)]
            for i in range(j + 1, 8):
                for n in range(j + 1, i + 1):
                    elem[i][n] = elem[i][n] - mult[i] * elem[n][j]
                for n in range(j):
                    inv[i][n] = inv[i][n] - mult[i] * inv[j][n]
                inv[i][j] = -mult[i]
        lrows = [wide(left[k][j:j + 1]) for j in range(8)]
        rrows = [wide(right[k][j:j + 1]) for j in range(8)]

        def solved(rows):
            first = []
            for j in range(8):
                total = rows[j]
                for n in range(j):
                    total = total + inv[j][n] * rows[n]
                first.append(total)
            scaled = [first[j] * pivots[j] for j in range(8)]
            second = []
            for j in range(8):
                total = scaled[j]
                for n in range(j + 1, 8):
                    total = total + inv[n][j] * scaled[n]
                second.append(total)
            return first, second

        unused, lsol = solved(lrows)
        rfirst, rsol = solved(rrows)
        for i in range(k + 1, 16):
            for j in range(8):
                f = wide(left[i][:, c + j:c + j + 1])
                left[i] = left[i] - f * lsol[j]
                right[i] = right[i] - f * rsol[j]
        rows = jnp.zeros((8, BS), F32)
        for j in range(8):
            rows = jnp.where(sub == j, rfirst[j] * roots[j], rows)
        out.append(rows)
        if k in (3, 11):
            yield None
    yield jnp.concatenate(out, axis=0)


def step_kernel(inverse, x_hbm, w_hbm, row_hbm, col_hbm, cnt_ref, search_hbm, proj_hbm,
                x_ref, row_ref, col_ref, search_ref, proj_ref, w_ref,
                slab1a, slab1b, slab2a, slab2b, prod, xt_ref, ints_v, floats_v, ints_s, floats_s,
                siba_s, siba_r, sibb_s, sibb_r, hi_s, hi_r, lo_s, lo_r, deg_s, deg_r,
                lap_ref, deg_ref, x_group, l_group,
                a_part, a_r1, a_b2, a_b3, a_res, b_part, b_r1, b_b2, b_res,
                send_sem, recv_sem, local_sem):
    slab1, slab2 = (slab1a, slab1b), (slab2a, slab2b)
    sib_s, sib_r = (siba_s, sibb_s), (siba_r, sibb_r)
    a = lax.axis_index("rows")
    b = lax.axis_index("cols")
    y, z = a // NZ, a % NZ
    xx, core = b // 2, b % 2
    counter = [0]

    def ydev(d):
        return {"rows": ((y + d + NY) % NY) * NZ + z, "cols": b}

    def zdev(d):
        return {"rows": y * NZ + (z + d + NZ) % NZ, "cols": b}

    def yzdev(d):
        return {"rows": ((y + d // NZ) % NY) * NZ + (z + d % NZ) % NZ, "cols": b}

    def coldev(d):
        return {"rows": a, "cols": (b + d) % NCOL}

    def xdev(d):
        return {"rows": a, "cols": ((xx + d) % NX) * 2 + core}

    sibling = {"rows": a, "cols": xx * 2 + (1 - core)}
    sent = [0]

    def new_sem():
        counter[0] += 1
        return counter[0] - 1

    def remote(src, dst, device, k):
        return pltpu.make_async_remote_copy(
            src_ref=src, dst_ref=dst, send_sem=send_sem.at[0], recv_sem=recv_sem.at[k],
            device_id=device, device_id_type=pl.DeviceIdType.MESH)

    def send(src, dst, device, k=None):
        copy = remote(src, dst, device, new_sem() if k is None else k)
        copy.start()
        sent[0] += math.prod(src.shape) * src.dtype.itemsize
        return copy

    def wait_bytes(like, k):
        remote(like, like, sibling, k).wait_recv()

    barrier = pltpu.get_barrier_semaphore()
    partners = [coldev(d) for d in range(1, NCOL)] + [yzdev(d) for d in range(1, NY * NZ)]
    for device in partners:
        pl.semaphore_signal(barrier, inc=1, device_id=device, device_id_type=pl.DeviceIdType.MESH)

    x_copy = pltpu.make_async_copy(x_hbm, x_ref, local_sem.at[3])
    row_copy = pltpu.make_async_copy(row_hbm, row_ref, local_sem.at[4])
    col_copy = pltpu.make_async_copy(col_hbm, col_ref, local_sem.at[5])
    x_copy.start()
    row_copy.start()
    col_copy.start()
    w_copies = [pltpu.make_async_copy(w_hbm.at[pl.ds(n * PART, PART)], w_ref.at[pl.ds(n * PART, PART)],
                                      local_sem.at[6 + n]) for n in range(SLOTS // PART)]
    for copy in w_copies:
        copy.start()
    x_copy.wait()

    place = ((z, y), (y, z))

    def span(p, i, j, size):
        return pl.ds(p * 32 + (i * 4 + j) * 2, size)

    for r in range(4):
        xt = x_ref[r * BS:(r + 1) * BS, :].astype(F32).T
        xt_ref[r] = xt
        xt = xt.astype(BF16)
        x_group[core, xx, r] = xt
        p, t = r // 2, r % 2
        for h in range(2):
            slab1[h][p * 32 + (place[p][0] * 4 + place[p][1]) * 2 + t] = xt[h * HALF:(h + 1) * HALF]
    w_ref[SLOTS] = jnp.zeros((BS, BS), BF16)
    pl.semaphore_wait(barrier, len(partners))

    def gather(slab):
        def first(p, d):
            return ydev(d) if p == 0 else zdev(d)

        def second(p, d):
            return zdev(d) if p == 0 else ydev(d)

        def block(p, i, j):
            return slab.at[span(p, i, j, 2)]

        def half(p, i, j, t):
            return slab.at[pl.ds(p * 32 + (i * 4 + j) * 2 + t, 1)]

        def spread(p, j):
            i = place[p][0]
            ref = block(p, i, j)
            return send(ref, ref, second(p, 1)), send(ref, ref, second(p, -1))

        def pass_on(p, j, pair, k):
            i = place[p][0]
            pair[0].wait_recv()
            one = half(p, (i + 3) % 4, j, 0)
            send(one, one, second(p, 1), k)
            pair[1].wait_recv()
            two = half(p, (i + 1) % 4, j, 1)
            send(two, two, second(p, -1), k)

        near, own, side, far = [], [], [], []
        ends = new_sem()
        for p in range(2):
            i, j = place[p]
            ref = block(p, i, j)
            near.append((send(ref, ref, first(p, 1)), send(ref, ref, first(p, -1))))
        for p in range(2):
            i, j = place[p]
            ref = block(p, i, j)
            far.append(send(ref, ref, first(p, 2)))
        for p in range(2):
            own.append(spread(p, place[p][1]))
        yield
        for p in range(2):
            j = place[p][1]
            near[p][0].wait_recv()
            one = spread(p, (j + 3) % 4)
            near[p][1].wait_recv()
            side.append((one, spread(p, (j + 1) % 4)))
        yield
        for p in range(2):
            i, j = place[p]
            far[p].wait_recv()
            ref = block(p, i, (j + 2) % 4)
            for d in (2, 1, -1):
                send(ref, ref, second(p, d), ends)
        yield
        for p in range(2):
            pass_on(p, place[p][1], own[p], ends)
        yield
        for p in range(2):
            pass_on(p, (place[p][1] + 3) % 4, side[p][0], ends)
            pass_on(p, (place[p][1] + 1) % 4, side[p][1], ends)
        yield
        wait_bytes(slab.at[pl.ds(0, 24)], ends)
        yield

    def group_gather(buf):
        copies = [send(buf.at[core, xx], buf.at[core, xx], xdev(d)) for d in (2, 1, 3)]
        yield
        for copy in copies:
            copy.wait_recv()
        copy = send(buf.at[core], buf.at[core], sibling)
        yield
        copy.wait_recv()
        yield

    g1 = [gather(slab1[h]) for h in range(2)]
    next(g1[0])
    row_copy.wait()
    col_copy.wait()
    ints, floats = sort_slots(row_ref[...], col_ref[...], cnt_ref[0, 0], a)
    ints_v[...] = ints
    floats_v[...] = floats
    ints_copy = pltpu.make_async_copy(ints_v, ints_s, local_sem.at[1])
    floats_copy = pltpu.make_async_copy(floats_v, floats_s, local_sem.at[2])
    ints_copy.start()
    floats_copy.start()
    def flip(n):
        def body(s, carry):
            w_ref[s] = w_ref[s].T
            return carry

        w_copies[n].wait()
        lax.fori_loop(n * PART, (n + 1) * PART, body, 0, unroll=16)

    flip(0)
    next(g1[0])
    next(g1[1])
    flip(1)
    next(g1[0])
    next(g1[0])
    flip(2)
    next(g1[0])
    next(g1[1])
    flip(3)
    next(g1[1])
    next(g1[1])
    ints_copy.wait()
    floats_copy.wait()
    xx_mat = sum(nt(xt_ref[r].astype(BF16), xt_ref[r].astype(BF16)) for r in range(4))
    a_part[:, 0] = xx_mat.reshape(8, 16, BS)
    next(g1[0])

    def pick(kind, at, top):
        return jnp.clip(ints_s[kind, at], 0, top)

    def product(slab, h, with_degree, hooks):
        rows = HALF + DEG if with_degree else HALF
        ones = jnp.ones((16, 2 * BS), BF16)

        def body(n, acc):
            for u in range(UNROLL):
                s = n * UNROLL + u
                left = jnp.concatenate([slab[pick(1, 2 * s, 63)], slab[pick(1, 2 * s + 1, 63)]], axis=1)
                if with_degree:
                    left = jnp.concatenate([left, ones], axis=0)
                right = jnp.concatenate([w_ref[pick(0, 2 * s, SLOTS)], w_ref[pick(0, 2 * s + 1, SLOTS)]], axis=0)
                acc = acc * floats_s[0, s] + nn(left, right)[:rows]
                prod[h, s, :rows] = acc
            return acc

        acc = jnp.zeros((rows, BS), F32)
        at = 0
        for step, hook in hooks + [(PAIRS // UNROLL, None)]:
            acc = lax.fori_loop(at, step, body, acc)
            at = step
            if hook is not None:
                hook()

    def tile(h, g, rows):
        return prod[h, pick(2, g, PAIRS - 1), :rows] * floats_s[1, g]

    def order(d):
        return (xx + d) % NX

    def joined(ref):
        return jnp.concatenate([ref[r] for r in range(4)], axis=1)

    def halves(h):
        return pl.ds(h * HALF, HALF)

    from_sib, hi_copy, deg_copy, lo_copy = {}, {}, {}, {}

    def reduce_start(h):
        rows = HALF + DEG if h == 0 else HALF
        for d in (2, 1, 3, 0):
            for r in range(4):
                sib_s[h][d, r] = tile(h, (order(d) * 2 + (1 - core)) * 4 + r, rows)
            from_sib[h, d] = send(sib_s[h].at[d], sib_r[h].at[d], sibling)

    def reduce_middle(h):
        rows = HALF + DEG if h == 0 else HALF
        for d in (2, 1, 3, 0):
            from_sib[h, d].wait_recv()
            for r in range(4):
                total = tile(h, (order(d) * 2 + core) * 4 + r, rows) + sib_r[h][d, r]
                if d:
                    high = total[:HALF].astype(BF16)
                    hi_s[h, d - 1, r] = high
                    lo_s[h, d - 1, r] = (total[:HALF] - high.astype(F32)).astype(BF16)
                    if h == 0:
                        deg_s[d - 1, r] = total[HALF:]
                else:
                    lap_ref[r, halves(h)] = total[:HALF]
                    if h == 0:
                        deg_ref[r] = total[HALF:]
            if d:
                if h == 0:
                    deg_copy[d] = send(deg_s.at[d - 1], deg_r.at[d - 1], xdev(d))
                hi_copy[h, d] = send(hi_s.at[h, d - 1], hi_r.at[h, d - 1], xdev(d))

    def reduce_end(h):
        for d in (1, 3, 2):
            if h == 0:
                deg_copy[d].wait_recv()
            hi_copy[h, d].wait_recv()
        for r in range(4):
            if h == 0:
                deg_ref[r] = deg_ref[r] + deg_r[0, r] + deg_r[1, r] + deg_r[2, r]
            degree = jnp.broadcast_to(deg_ref[r][:1], (HALF, BS))
            summed = lap_ref[r, halves(h)] + sum(hi_r[h, d, r].astype(F32) for d in range(3))
            lap = degree * xt_ref[r, halves(h)] - summed
            lap_ref[r, halves(h)] = lap
            lap = lap.astype(BF16)
            l_group[core, xx, r, halves(h)] = lap
            p, t = r // 2, r % 2
            slab2[h][p * 32 + (place[p][0] * 4 + place[p][1]) * 2 + t] = lap

    def all_reduce(part, r1, b2, b3, res):
        sems = [new_sem() for unused in range(4)]
        for d in range(1, NCOL):
            send(part.at[(b + d) % NCOL], r1.at[d - 1], coldev(d), sems[0])
        yield
        wait_bytes(r1, sems[0])
        total = part[b]
        for d in range(1, NCOL):
            total = total + r1[d - 1]
        b2[y] = total
        for d in (1, 2, 3):
            send(b2.at[y], b2.at[y], ydev(d), sems[1])
        yield
        wait_bytes(b2.at[pl.ds(0, 3)], sems[1])
        b3[z] = b2[0] + b2[1] + b2[2] + b2[3]
        for d in (1, 2, 3):
            send(b3.at[z], b3.at[z], zdev(d), sems[2])
        yield
        wait_bytes(b3.at[pl.ds(0, 3)], sems[2])
        res[b] = b3[0] + b3[1] + b3[2] + b3[3]
        for d in range(1, NCOL):
            send(res.at[b], res.at[b], coldev(d), sems[3])
        yield
        wait_bytes(res.at[pl.ds(0, 7)], sems[3])
        yield

    xg = group_gather(x_group)
    next(xg)
    product(slab1[0], 0, True, [(1, lambda: next(g1[1]))])
    reduce_start(0)
    next(g1[1])

    def middle():
        reduce_middle(0)
        next(xg)

    product(slab1[1], 1, False, [(2, middle)])
    reduce_start(1)
    reduce_end(0)
    g2 = [gather(slab2[h]) for h in range(2)]
    next(g2[0])
    reduce_middle(1)
    next(g2[0])
    next(g2[0])
    reduce_end(1)
    next(g2[1])
    lap_all = joined(lap_ref)
    a_part[:, 1] = nt(joined(xt_ref), lap_all, HI).reshape(8, 16, BS)
    a_part[:, 2] = nt(lap_all, lap_all, HI).reshape(8, 16, BS)
    reduce_a = all_reduce(a_part, a_r1, a_b2, a_b3, a_res)
    next(reduce_a)
    lg = group_gather(l_group)
    next(lg)
    next(g2[0])
    next(g2[0])
    scaled = joined(lap_ref) * jnp.concatenate([jnp.broadcast_to(deg_ref[r][:1], (BS, BS)) for r in range(4)], axis=1)
    pair_rows = jnp.concatenate([joined(xt_ref), joined(lap_ref)], axis=0)
    b_part[...] = nt(scaled, pair_rows, HI).reshape(8, 16, 2 * BS)
    next(g2[1])
    next(g2[1])
    next(g2[1])
    next(reduce_a)
    next(g2[0])

    def early():
        next(g2[1])
        for h in range(2):
            for d in (2, 1, 3):
                lo_copy[h, d] = send(lo_s.at[h, d - 1], lo_r.at[h, d - 1], xdev(d))

    product(slab2[0], 0, False, [(1, early), (3, lambda: next(reduce_a))])
    next(lg)
    next(g2[1])
    next(reduce_a)
    product(slab2[1], 1, False, [])
    next(lg)
    next(xg)
    total = jnp.zeros((BS, 2 * BS), F32)
    for c in range(2):
        for k in range(4):
            for r in (0, 2):
                g = (k * 2 + c) * 4 + r
                part = jnp.concatenate(
                    [jnp.concatenate([tile(h, g, HALF), tile(h, g + 1, HALF)], axis=1) for h in range(2)], axis=0)
                top = jnp.concatenate([x_group[c, k, r], x_group[c, k, r + 1]], axis=1)
                low = jnp.concatenate([l_group[c, k, r], l_group[c, k, r + 1]], axis=1)
                total = total + nt(part.astype(BF16), jnp.concatenate([top, low], axis=0))
    b_part[...] = b_part[...] - total.reshape(8, 16, 2 * BS)
    sems_b = [new_sem() for unused in range(3)]
    for d in range(1, NCOL):
        send(b_part.at[(b + d) % NCOL], b_r1.at[d - 1], coldev(d), sems_b[0])
    next(reduce_a)
    def mat(m):
        return a_res[:, m].reshape(BS, BS) * inverse

    gx, theta, s_mat = mat(0), mat(1), mat(2)
    m = 2.0 * theta - nn(gx, theta, HI)
    m_t = m.T
    cross = nn(m_t, theta, HI)
    gram = s_mat - cross.T - cross + nn(m_t, nn(gx, m, HI), HI)
    factor = factor_inverse(gram)
    next(factor)
    wait_bytes(b_r1, sems_b[0])
    part = b_part[b]
    for d in range(1, NCOL):
        part = part + b_r1[d - 1]
    b_b2[a] = part
    for d in range(1, NY * NZ):
        send(b_b2.at[a], b_b2.at[a], yzdev(d), sems_b[1])
    next(factor)
    wait_bytes(b_b2.at[pl.ds(0, NY * NZ - 1)], sems_b[1])
    part = b_b2[0]
    for k in range(1, NY * NZ):
        part = part + b_b2[k]
    b_res[b] = part
    for d in range(1, NCOL):
        send(b_res.at[b], b_res.at[b], coldev(d), sems_b[2])
    t_t = next(factor)
    for h in range(2):
        for d in (1, 3, 2):
            lo_copy[h, d].wait_recv()
    mt_t = nt(t_t, m, HI)
    for r in range(4):
        low = [sum(lo_r[h, d, r].astype(F32) for d in range(3)) for h in range(2)]
        lap = lap_ref[r] - jnp.concatenate(low, axis=0)
        part = nn(t_t, lap, HI) - nn(mt_t, xt_ref[r], HI)
        search_ref[r * BS:(r + 1) * BS, :] = part.T.astype(BF16)
    search_copy = pltpu.make_async_copy(search_ref, search_hbm, local_sem.at[3])
    search_copy.start()
    e1 = nt(mt_t, theta, HI)
    e2 = nn(mt_t, s_mat, HI)
    tail = jnp.concatenate([t_t, -mt_t], axis=1)
    proj_ref[:BS, :BS] = theta
    proj_ref[BS:, :BS] = nn(t_t, s_mat - cross, HI)
    wait_bytes(b_res.at[pl.ds(0, 7)], sems_b[2])
    spun = nn(t_t, b_res[...].reshape(BS, 2 * BS) * inverse, HI)
    xq = spun[:, :BS] - e1
    qq = nt(jnp.concatenate([spun[:, BS:] - e2, xq], axis=1), tail, HI)
    proj_ref[:BS, BS:] = xq.T
    proj_ref[BS:, BS:] = qq.T
    proj_copy = pltpu.make_async_copy(proj_ref, proj_hbm, local_sem.at[4])
    proj_copy.start()
    assert counter[0] <= N_SEM
    whole = w_ref.at[pl.ds(0, sent[0] // BLOCK_BYTES)]
    assert sent[0] % BLOCK_BYTES == 0
    remote(whole, whole, sibling, 0).wait_send()
    search_copy.wait()
    proj_copy.wait()


def shards(iterate, blocks, block_row, block_col, block_count):
    shape = jax.ShapeDtypeStruct
    rows1 = HALF + DEG
    node_total = iterate.shape[0] * lax.axis_size("rows") * lax.axis_size("cols")

    def buf(*dims, dtype=F32):
        return pltpu.VMEM(dims, dtype)

    def kernel(*refs):
        step_kernel(1.0 / node_total, *refs)

    outs = (shape(iterate.shape, BF16), shape((2 * BS, 2 * BS), F32))
    hbm = pl.BlockSpec(memory_space=pl.ANY)
    search, projected = pl.pallas_call(
        kernel,
        out_shape=outs,
        in_specs=[hbm, hbm, hbm, hbm, pl.BlockSpec(memory_space=pltpu.SMEM)],
        out_specs=(hbm, hbm),
        scratch_shapes=[
            buf(4 * BS, BS, dtype=BF16), buf(1, SLOTS, dtype=jnp.int32), buf(1, SLOTS, dtype=jnp.int32),
            buf(4 * BS, BS, dtype=BF16), buf(2 * BS, 2 * BS),
            buf(SLOTS + 1, BS, BS, dtype=BF16),
            buf(64, HALF, BS, dtype=BF16), buf(64, HALF, BS, dtype=BF16),
            buf(64, HALF, BS, dtype=BF16), buf(64, HALF, BS, dtype=BF16),
            buf(2, PAIRS, rows1, BS), buf(4, BS, BS), buf(8, 512, dtype=jnp.int32), buf(8, 512),
            pltpu.SMEM((8, 512), jnp.int32), pltpu.SMEM((8, 512), F32),
            buf(4, 4, rows1, BS), buf(4, 4, rows1, BS), buf(4, 4, HALF, BS), buf(4, 4, HALF, BS),
            buf(2, 3, 4, HALF, BS, dtype=BF16), buf(2, 3, 4, HALF, BS, dtype=BF16),
            buf(2, 3, 4, HALF, BS, dtype=BF16), buf(2, 3, 4, HALF, BS, dtype=BF16),
            buf(3, 4, DEG, BS), buf(3, 4, DEG, BS),
            buf(4, BS, BS), buf(4, DEG, BS),
            buf(2, 4, 4, BS, BS, dtype=BF16), buf(2, 4, 4, BS, BS, dtype=BF16),
            buf(8, 3, 16, BS), buf(7, 3, 16, BS), buf(4, 3, 16, BS), buf(4, 3, 16, BS), buf(8, 3, 16, BS),
            buf(8, 16, 2 * BS), buf(7, 16, 2 * BS), buf(16, 16, 2 * BS), buf(8, 16, 2 * BS),
            pltpu.SemaphoreType.DMA((1,)), pltpu.SemaphoreType.DMA((N_SEM,)), pltpu.SemaphoreType.DMA((10,)),
        ],
        compiler_params=pltpu.CompilerParams(
            collective_id=0, has_side_effects=True, vmem_limit_bytes=60 * 1024 * 1024),
        name="lobpcg_step",
    )(iterate, blocks.reshape(SLOTS, BS, BS), block_row.reshape(1, SLOTS), block_col.reshape(1, SLOTS),
      block_count.reshape(1, 1))

    def hand_over(search_ref, projected_ref, search_out, projected_out, search_v, projected_v, sems):
        pairs = [(search_ref, search_v, search_out), (projected_ref, projected_v, projected_out)]
        reads = [pltpu.make_async_copy(src, mid, sems.at[n]) for n, (src, mid, dst) in enumerate(pairs)]
        writes = [pltpu.make_async_copy(mid, dst, sems.at[n + 2]) for n, (src, mid, dst) in enumerate(pairs)]
        for copy in reads:
            copy.start()
        for n in range(2):
            reads[n].wait()
            writes[n].start()
        for copy in writes:
            copy.wait()

    return pl.pallas_call(
        hand_over, out_shape=outs, in_specs=[hbm, hbm], out_specs=(hbm, hbm),
        scratch_shapes=[buf(4 * BS, BS, dtype=BF16), buf(2 * BS, 2 * BS), pltpu.SemaphoreType.DMA((4,))],
        name="hand_over",
    )(search, projected)


def solution(mesh):
    placed = (
        P(("rows", "cols"), None),
        P("rows", "cols", None, None, None),
        P("rows", "cols", None),
        P("rows", "cols", None),
        P("rows", "cols"),
    )
    return jax.shard_map(
        shards,
        mesh=mesh,
        in_specs=placed,
        out_specs=(P(("rows", "cols"), None), P()),
        check_vma=False,
    )
```

```python
import math

import jax
import jax.numpy as jnp
from jax import lax
from jax.experimental import pallas as pl
from jax.experimental.pallas import tpu as pltpu
from jax.sharding import PartitionSpec as P

BS = 128
NY = 4
NZ = 4
NX = 4
NCOL = 8
GROUP = 32
SLOTS = 384
PAIRS = (SLOTS + GROUP) // 2
UNROLL = 52
PART = 96
DEG = 8
N_SEM = 120
HALF = BS // 2
BLOCK_BYTES = BS * BS * 2

F32 = jnp.float32
BF16 = jnp.bfloat16
HI = lax.Precision.HIGHEST


def nt(a, b, precision=None):
    return lax.dot_general(a, b, (((1,), (1,)), ((), ())), precision=precision, preferred_element_type=F32)


def nn(a, b, precision=None):
    return jnp.dot(a, b, precision=precision, preferred_element_type=F32)


def iota(shape, dim):
    return lax.broadcasted_iota(jnp.int32, shape, dim)


def flag(mask):
    return jnp.where(mask, 1.0, 0.0).astype(F32)


def sort_slots(row, col, count, a):
    live = iota((1, SLOTS), 1) < count
    local = jnp.where(live, row - a * GROUP, 2 * GROUP - 1)
    owner = col >> 5
    part = col & 3
    oy, oz = owner >> 2, owner & 3
    piece = part >> 1
    place = jnp.where(piece == 0, oz * 4 + oy, oy * 4 + oz)
    tile = piece * 32 + place * 2 + (part & 1)
    local_f = local.astype(F32)
    row_t = jnp.broadcast_to(local_f, (BS, SLOTS)).T
    lane = iota((SLOTS, BS), 1).astype(F32)
    hits = flag(row_t == lane)
    counts = jnp.sum(hits, axis=0, keepdims=True)
    counts = jnp.where(iota((1, BS), 1) < GROUP, counts, 0.0)
    pairs = ((counts.astype(jnp.int32) + 1) >> 1).astype(F32)
    upper = flag(iota((BS, BS), 0) < iota((BS, BS), 1)).astype(BF16)
    start = nn(jnp.broadcast_to(pairs, (16, BS)).astype(BF16), upper)[:1]
    row_w = jnp.concatenate([row_t] * (SLOTS // BS), axis=1)
    before = (row_w == local_f) & (iota((SLOTS, SLOTS), 1) < iota((SLOTS, SLOTS), 0))
    within = jnp.sum(flag(before), axis=1, keepdims=True)
    base = jnp.sum(hits * start, axis=1, keepdims=True)
    pos = 2.0 * base + within
    pos = jnp.where(row_t[:, :1] < GROUP, pos, 4096.0)
    onehot = flag(pos == iota((SLOTS, 512), 1).astype(F32)).astype(BF16)
    slot = iota((1, SLOTS), 1)
    values = jnp.concatenate(
        [(slot >> 4).astype(F32), (slot & 15).astype(F32), tile.astype(F32), jnp.ones((1, SLOTS), F32),
         jnp.zeros((12, SLOTS), F32)], axis=0).astype(BF16)
    placed = nn(values, onehot)
    perm = placed[0:1] * 16.0 + placed[1:2] + SLOTS * (1.0 - placed[3:4])
    start_t = jnp.broadcast_to(start, (BS, BS)).T
    pairs_t = jnp.broadcast_to(pairs, (BS, BS)).T
    lane4 = iota((BS, 512), 1).astype(F32)
    first = jnp.sum(flag((start_t[:, :1] == lane4) & (pairs_t[:, :1] > 0.0)), axis=0, keepdims=True)
    pad = jnp.zeros((1, 512 - BS), F32)
    last = jnp.concatenate([jnp.maximum(start + pairs - 1.0, 0.0), pad], axis=1)
    filled = jnp.concatenate([jnp.minimum(pairs, 1.0), pad], axis=1)
    ints = jnp.concatenate([perm, placed[2:3], last, jnp.zeros((5, 512), F32)], axis=0).astype(jnp.int32)
    floats = jnp.concatenate([1.0 - first, filled, jnp.zeros((6, 512), F32)], axis=0)
    return ints, floats


def half_inverse(block):
    both = jnp.concatenate([block, flag(iota((HALF, HALF), 0) == iota((HALF, HALF), 1))], axis=1)
    rows = [both[8 * i:8 * i + 8] for i in range(8)]
    sub = iota((8, BS), 0)
    out = []

    def wide(v):
        return jnp.broadcast_to(v, (8, BS))

    for k in range(8):
        c = 8 * k
        lanes = [wide(rows[k][:, c + n:c + n + 1]) for n in range(8)]
        elem = [[wide(lanes[n][j:j + 1]) if n <= j else None for n in range(8)] for j in range(8)]
        inv = [[None] * 8 for unused in range(8)]
        roots, pivots = [], []
        for j in range(8):
            root = lax.rsqrt(elem[j][j])
            roots.append(root)
            pivots.append(root * root)
            mult = [elem[i][j] * pivots[j] if i > j else None for i in range(8)]
            for i in range(j + 1, 8):
                for n in range(j + 1, i + 1):
                    elem[i][n] = elem[i][n] - mult[i] * elem[n][j]
                for n in range(j):
                    inv[i][n] = inv[i][n] - mult[i] * inv[j][n]
                inv[i][j] = -mult[i]
        held = [wide(rows[k][j:j + 1]) for j in range(8)]
        first = []
        for j in range(8):
            total = held[j]
            for n in range(j):
                total = total + inv[j][n] * held[n]
            first.append(total)
        if k < 7:
            scaled = [first[j] * pivots[j] for j in range(8)]
            solved = []
            for j in range(8):
                total = scaled[j]
                for n in range(j + 1, 8):
                    total = total + inv[n][j] * scaled[n]
                solved.append(total)
            factors = [[wide(rows[i][:, c + j:c + j + 1]) for j in range(8)] for i in range(k + 1, 8)]
            for i in range(k + 1, 8):
                for j in range(8):
                    rows[i] = rows[i] - factors[i - k - 1][j] * solved[j]
        done = jnp.zeros((8, BS), F32)
        for j in range(8):
            done = jnp.where(sub == j, first[j] * roots[j], done)
        out.append(done)
    return jnp.concatenate(out, axis=0)[:, HALF:]


def step_kernel(inverse, x_hbm, w_hbm, row_hbm, col_hbm, cnt_ref, search_hbm, proj_hbm,
                x_ref, row_ref, col_ref, search_ref, proj_ref, w_ref,
                slab1a, slab1b, slab2a, slab2b, prod, xt_ref, ints_v, floats_v, ints_s, floats_s,
                siba_s, siba_r, sibb_s, sibb_r, hi_s, hi_r, lo_s, lo_r, deg_s, deg_r,
                lap_ref, deg_ref, x_group, l_group,
                a_part, a_r1, a_b2, a_b3, a_res, b_part, b_r1, b_b2, b_res,
                fence_ref, send_sem, recv_sem, local_sem):
    slab1, slab2 = (slab1a, slab1b), (slab2a, slab2b)
    sib_s, sib_r = (siba_s, sibb_s), (siba_r, sibb_r)
    a = lax.axis_index("rows")
    b = lax.axis_index("cols")
    y, z = a // NZ, a % NZ
    xx, core = b // 2, b % 2
    counter = [0]
    never = jnp.where(a >= NY * NZ, 1, 0)

    def fence():
        def body(unused, carry):
            fence_ref[...] = jnp.zeros_like(fence_ref)
            return carry

        lax.fori_loop(0, never, body, 0)


    def ydev(d):
        return {"rows": ((y + d + NY) % NY) * NZ + z, "cols": b}

    def zdev(d):
        return {"rows": y * NZ + (z + d + NZ) % NZ, "cols": b}

    def yzdev(d):
        return {"rows": ((y + d // NZ) % NY) * NZ + (z + d % NZ) % NZ, "cols": b}

    def coldev(d):
        return {"rows": a, "cols": (b + d) % NCOL}

    def xdev(d):
        return {"rows": a, "cols": ((xx + d) % NX) * 2 + core}

    sibling = {"rows": a, "cols": xx * 2 + (1 - core)}
    sent = [0]

    def new_sem():
        counter[0] += 1
        return counter[0] - 1

    def remote(src, dst, device, k):
        return pltpu.make_async_remote_copy(
            src_ref=src, dst_ref=dst, send_sem=send_sem.at[0], recv_sem=recv_sem.at[k],
            device_id=device, device_id_type=pl.DeviceIdType.MESH)

    def send(src, dst, device, k=None):
        copy = remote(src, dst, device, new_sem() if k is None else k)
        copy.start()
        sent[0] += math.prod(src.shape) * src.dtype.itemsize
        return copy

    def wait_bytes(like, k):
        remote(like, like, sibling, k).wait_recv()

    barrier = pltpu.get_barrier_semaphore()
    partners = [coldev(d) for d in range(1, NCOL)] + [yzdev(d) for d in range(1, NY * NZ)]
    for device in partners:
        pl.semaphore_signal(barrier, inc=1, device_id=device, device_id_type=pl.DeviceIdType.MESH)

    x_copy = pltpu.make_async_copy(x_hbm, x_ref, local_sem.at[3])
    row_copy = pltpu.make_async_copy(row_hbm, row_ref, local_sem.at[4])
    col_copy = pltpu.make_async_copy(col_hbm, col_ref, local_sem.at[5])
    x_copy.start()
    row_copy.start()
    col_copy.start()
    w_copies = [pltpu.make_async_copy(w_hbm.at[pl.ds(n * PART, PART)], w_ref.at[pl.ds(n * PART, PART)],
                                      local_sem.at[6 + n]) for n in range(SLOTS // PART)]
    for copy in w_copies:
        copy.start()
    x_copy.wait()

    place = ((z, y), (y, z))

    def span(p, i, j, size):
        return pl.ds(p * 32 + (i * 4 + j) * 2, size)

    for r in range(4):
        xt = x_ref[r * BS:(r + 1) * BS, :].astype(F32).T
        xt_ref[r] = xt
        xt = xt.astype(BF16)
        x_group[core, xx, r] = xt
        p, t = r // 2, r % 2
        for h in range(2):
            slab1[h][p * 32 + (place[p][0] * 4 + place[p][1]) * 2 + t] = xt[h * HALF:(h + 1) * HALF]
    w_ref[SLOTS] = jnp.zeros((BS, BS), BF16)
    fence()
    pl.semaphore_wait(barrier, len(partners))

    def gather(slab, direct):
        def first(p, d):
            return ydev(d) if p == 0 else zdev(d)

        def second(p, d):
            return zdev(d) if p == 0 else ydev(d)

        def block(p, i, j):
            return slab.at[span(p, i, j, 2)]

        def half(p, i, j, t):
            return slab.at[pl.ds(p * 32 + (i * 4 + j) * 2 + t, 1)]

        def spread(p, j):
            i = place[p][0]
            ref = block(p, i, j)
            return send(ref, ref, second(p, 1)), send(ref, ref, second(p, -1))

        def pass_on(p, j, pair, k):
            i = place[p][0]
            pair[0].wait_recv()
            one = half(p, (i + 3) % 4, j, 0)
            send(one, one, second(p, 1), k)
            pair[1].wait_recv()
            two = half(p, (i + 1) % 4, j, 1)
            send(two, two, second(p, -1), k)

        def spread_all(p, j):
            ref = block(p, place[p][0], j)
            for d in (2, 1, -1):
                send(ref, ref, second(p, d), ends)

        near, own, side, far = [], [], [], []
        ends = new_sem()
        for p in range(2):
            i, j = place[p]
            ref = block(p, i, j)
            near.append((send(ref, ref, first(p, 1)), send(ref, ref, first(p, -1))))
        for p in range(2):
            i, j = place[p]
            ref = block(p, i, j)
            far.append(send(ref, ref, first(p, 2)))
        if direct:
            for p in range(2):
                spread_all(p, place[p][1])
            yield
            for p in range(2):
                for n, j in enumerate((3, 1)):
                    near[p][n].wait_recv()
                    spread_all(p, (place[p][1] + j) % 4)
            yield
            for p in range(2):
                far[p].wait_recv()
                spread_all(p, (place[p][1] + 2) % 4)
            yield
            wait_bytes(slab.at[pl.ds(0, 48)], ends)
            yield
            return
        for p in range(2):
            own.append(spread(p, place[p][1]))
        yield
        for p in range(2):
            j = place[p][1]
            near[p][0].wait_recv()
            one = spread(p, (j + 3) % 4)
            near[p][1].wait_recv()
            side.append((one, spread(p, (j + 1) % 4)))
        yield
        for p in range(2):
            far[p].wait_recv()
            spread_all(p, (place[p][1] + 2) % 4)
        yield
        for p in range(2):
            pass_on(p, place[p][1], own[p], ends)
        yield
        for p in range(2):
            pass_on(p, (place[p][1] + 3) % 4, side[p][0], ends)
            pass_on(p, (place[p][1] + 1) % 4, side[p][1], ends)
        yield
        wait_bytes(slab.at[pl.ds(0, 24)], ends)
        yield

    def group_gather(buf):
        copies = [send(buf.at[core, xx], buf.at[core, xx], xdev(d)) for d in (2, 1, 3)]
        yield
        for copy in copies:
            copy.wait_recv()
        copy = send(buf.at[core], buf.at[core], sibling)
        yield
        copy.wait_recv()
        yield

    fence()
    g1 = [gather(slab1[h], h == 1) for h in range(2)]
    next(g1[0])
    fence()
    row_copy.wait()
    col_copy.wait()
    ints, floats = sort_slots(row_ref[...], col_ref[...], cnt_ref[0, 0], a)
    ints_v[...] = ints
    floats_v[...] = floats
    ints_copy = pltpu.make_async_copy(ints_v, ints_s, local_sem.at[1])
    floats_copy = pltpu.make_async_copy(floats_v, floats_s, local_sem.at[2])
    ints_copy.start()
    floats_copy.start()
    def flip(n):
        def body(s, carry):
            w_ref[s] = w_ref[s].T
            return carry

        w_copies[n].wait()
        lax.fori_loop(n * PART, (n + 1) * PART, body, 0, unroll=16)

    fence()
    flip(0)
    fence()
    next(g1[0])
    fence()
    next(g1[1])
    fence()
    flip(1)
    fence()
    next(g1[0])
    fence()
    next(g1[0])
    fence()
    flip(2)
    fence()
    next(g1[0])
    fence()
    next(g1[1])
    fence()
    flip(3)
    fence()
    next(g1[1])
    xg = group_gather(x_group)
    next(xg)
    fence()
    ints_copy.wait()
    floats_copy.wait()
    xx_mat = sum(nt(xt_ref[r].astype(BF16), xt_ref[r].astype(BF16)) for r in range(4))
    a_part[:, 0] = xx_mat.reshape(8, 16, BS)
    fence()
    next(g1[0])

    def pick(kind, at, top):
        return jnp.clip(ints_s[kind, at], 0, top)

    def product(slab, h, with_degree, hooks):
        rows = HALF + DEG if with_degree else HALF
        ones = jnp.ones((16, 2 * BS), BF16)

        def body(n, acc):
            for u in range(UNROLL):
                s = n * UNROLL + u
                left = jnp.concatenate([slab[pick(1, 2 * s, 63)], slab[pick(1, 2 * s + 1, 63)]], axis=1)
                if with_degree:
                    left = jnp.concatenate([left, ones], axis=0)
                right = jnp.concatenate([w_ref[pick(0, 2 * s, SLOTS)], w_ref[pick(0, 2 * s + 1, SLOTS)]], axis=0)
                acc = acc * floats_s[0, s] + nn(left, right)[:rows]
                prod[h, s, :rows] = acc
            return acc

        acc = jnp.zeros((rows, BS), F32)
        at = 0
        for step, hook in hooks + [(PAIRS // UNROLL, None)]:
            acc = lax.fori_loop(at, step, body, acc)
            at = step
            if hook is not None:
                hook()

    def tile(h, g, rows):
        return prod[h, pick(2, g, PAIRS - 1), :rows] * floats_s[1, g]

    def order(d):
        return (xx + d) % NX

    def joined(ref):
        return jnp.concatenate([ref[r] for r in range(4)], axis=1)

    def halves(h):
        return pl.ds(h * HALF, HALF)

    from_sib, hi_copy, deg_copy, lo_copy = {}, {}, {}, {}

    def reduce_start(h):
        rows = HALF + DEG if h == 0 else HALF
        for d in (2, 1, 3, 0):
            for r in range(4):
                sib_s[h][d, r] = tile(h, (order(d) * 2 + (1 - core)) * 4 + r, rows)
            from_sib[h, d] = send(sib_s[h].at[d], sib_r[h].at[d], sibling)

    def reduce_middle(h):
        rows = HALF + DEG if h == 0 else HALF
        for d in (2, 1, 3, 0):
            from_sib[h, d].wait_recv()
            for r in range(4):
                total = tile(h, (order(d) * 2 + core) * 4 + r, rows) + sib_r[h][d, r]
                if d:
                    high = total[:HALF].astype(BF16)
                    hi_s[h, d - 1, r] = high
                    lo_s[h, d - 1, r] = (total[:HALF] - high.astype(F32)).astype(BF16)
                    if h == 0:
                        deg_s[d - 1, r] = total[HALF:]
                else:
                    lap_ref[r, halves(h)] = total[:HALF]
                    if h == 0:
                        deg_ref[r] = total[HALF:]
            if d:
                if h == 0:
                    deg_copy[d] = send(deg_s.at[d - 1], deg_r.at[d - 1], xdev(d))
                hi_copy[h, d] = send(hi_s.at[h, d - 1], hi_r.at[h, d - 1], xdev(d))

    def reduce_end(h):
        for d in (1, 3, 2):
            if h == 0:
                deg_copy[d].wait_recv()
            hi_copy[h, d].wait_recv()
        for r in range(4):
            if h == 0:
                deg_ref[r] = deg_ref[r] + deg_r[0, r] + deg_r[1, r] + deg_r[2, r]
            degree = jnp.broadcast_to(deg_ref[r][:1], (HALF, BS))
            summed = lap_ref[r, halves(h)] + sum(hi_r[h, d, r].astype(F32) for d in range(3))
            lap = degree * xt_ref[r, halves(h)] - summed
            lap_ref[r, halves(h)] = lap
            lap = lap.astype(BF16)
            l_group[core, xx, r, halves(h)] = lap
            p, t = r // 2, r % 2
            slab2[h][p * 32 + (place[p][0] * 4 + place[p][1]) * 2 + t] = lap

    def all_reduce(part, r1, b2, b3, res):
        sems = [new_sem() for unused in range(4)]
        for d in range(1, NCOL):
            send(part.at[(b + d) % NCOL], r1.at[d - 1], coldev(d), sems[0])
        yield
        wait_bytes(r1, sems[0])
        total = part[b]
        for d in range(1, NCOL):
            total = total + r1[d - 1]
        b2[y] = total
        for d in (1, 2, 3):
            send(b2.at[y], b2.at[y], ydev(d), sems[1])
        yield
        wait_bytes(b2.at[pl.ds(0, 3)], sems[1])
        b3[z] = b2[0] + b2[1] + b2[2] + b2[3]
        for d in (1, 2, 3):
            send(b3.at[z], b3.at[z], zdev(d), sems[2])
        yield
        wait_bytes(b3.at[pl.ds(0, 3)], sems[2])
        res[b] = b3[0] + b3[1] + b3[2] + b3[3]
        for d in range(1, NCOL):
            send(res.at[b], res.at[b], coldev(d), sems[3])
        yield
        wait_bytes(res.at[pl.ds(0, 7)], sems[3])
        yield

    fence()
    product(slab1[0], 0, True, [])
    fence()
    reduce_start(0)
    fence()
    next(g1[1])

    fence()
    product(slab1[1], 1, False, [(1, lambda: reduce_middle(0))])
    next(xg)
    fence()
    reduce_start(1)
    fence()
    reduce_end(0)
    fence()
    g2 = [gather(slab2[h], h == 1) for h in range(2)]
    next(g2[0])
    fence()
    reduce_middle(1)
    fence()
    next(g2[0])
    fence()
    next(g2[0])
    fence()
    reduce_end(1)
    fence()
    next(g2[1])
    fence()
    lap_all = joined(lap_ref)
    a_part[:, 1] = nt(joined(xt_ref), lap_all, HI).reshape(8, 16, BS)
    a_part[:, 2] = nt(lap_all, lap_all, HI).reshape(8, 16, BS)
    reduce_a = all_reduce(a_part, a_r1, a_b2, a_b3, a_res)
    next(reduce_a)
    lg = group_gather(l_group)
    next(lg)
    fence()
    next(g2[0])
    fence()
    next(g2[0])
    fence()
    scaled = joined(lap_ref) * jnp.concatenate([jnp.broadcast_to(deg_ref[r][:1], (BS, BS)) for r in range(4)], axis=1)
    pair_rows = jnp.concatenate([joined(xt_ref), joined(lap_ref)], axis=0)
    b_part[...] = nt(scaled, pair_rows, HI).reshape(8, 16, 2 * BS)
    fence()
    next(g2[1])
    fence()
    next(g2[1])
    fence()
    next(reduce_a)
    fence()
    next(g2[0])

    def early():
        for h in range(2):
            for d in (2, 1, 3):
                lo_copy[h, d] = send(lo_s.at[h, d - 1], lo_r.at[h, d - 1], xdev(d))

    fence()
    product(slab2[0], 0, False, [(1, early)])
    fence()
    next(lg)
    fence()
    next(g2[1])
    fence()
    product(slab2[1], 1, False, [(1, lambda: next(reduce_a))])
    fence()
    next(lg)
    next(xg)
    fence()
    total = jnp.zeros((BS, 2 * BS), F32)
    for c in range(2):
        for k in range(4):
            for r in (0, 2):
                g = (k * 2 + c) * 4 + r
                part = jnp.concatenate(
                    [jnp.concatenate([tile(h, g, HALF), tile(h, g + 1, HALF)], axis=1) for h in range(2)], axis=0)
                top = jnp.concatenate([x_group[c, k, r], x_group[c, k, r + 1]], axis=1)
                low = jnp.concatenate([l_group[c, k, r], l_group[c, k, r + 1]], axis=1)
                total = total + nt(part.astype(BF16), jnp.concatenate([top, low], axis=0))
    b_part[...] = b_part[...] - total.reshape(8, 16, 2 * BS)
    fence()
    sems_b = [new_sem() for unused in range(3)]
    for d in range(1, NCOL):
        send(b_part.at[(b + d) % NCOL], b_r1.at[d - 1], coldev(d), sems_b[0])
    fence()
    next(reduce_a)
    fence()
    wait_bytes(b_r1, sems_b[0])
    part = b_part[b]
    for d in range(1, NCOL):
        part = part + b_r1[d - 1]
    b_b2[a] = part
    for d in range(1, NY * NZ):
        send(b_b2.at[a], b_b2.at[a], yzdev(d), sems_b[1])
    fence()
    next(reduce_a)
    fence()
    def mat(m):
        return a_res[:, m].reshape(BS, BS) * inverse

    gx, theta, s_mat = mat(0), mat(1), mat(2)
    m = 2.0 * theta - nn(gx, theta, HI)
    m_t = m.T
    cross = nn(m_t, theta, HI)
    gram = s_mat - cross.T - cross + nn(m_t, nn(gx, m, HI), HI)
    fence()
    inv_a = half_inverse(gram[:HALF, :HALF])
    side = nt(gram[HALF:, :HALF], inv_a, HI)
    fence()
    inv_c = half_inverse(gram[HALF:, HALF:] - nt(side, side, HI))
    corner = nn(inv_c, nn(side, inv_a, HI), HI)
    t_t = jnp.concatenate(
        [jnp.concatenate([inv_a, jnp.zeros((HALF, HALF), F32)], axis=1), jnp.concatenate([-corner, inv_c], axis=1)],
        axis=0)
    fence()
    wait_bytes(b_b2.at[pl.ds(0, NY * NZ - 1)], sems_b[1])
    part = b_b2[0]
    for k in range(1, NY * NZ):
        part = part + b_b2[k]
    b_res[b] = part
    for d in range(1, NCOL):
        send(b_res.at[b], b_res.at[b], coldev(d), sems_b[2])
    fence()
    for h in range(2):
        for d in (1, 3, 2):
            lo_copy[h, d].wait_recv()
    fence()
    mt_t = nt(t_t, m, HI)
    for r in range(4):
        low = [sum(lo_r[h, d, r].astype(F32) for d in range(3)) for h in range(2)]
        lap = lap_ref[r] - jnp.concatenate(low, axis=0)
        part = nn(t_t, lap, HI) - nn(mt_t, xt_ref[r], HI)
        search_ref[r * BS:(r + 1) * BS, :] = part.T.astype(BF16)
    search_copy = pltpu.make_async_copy(search_ref, search_hbm, local_sem.at[3])
    search_copy.start()
    e1 = nt(mt_t, theta, HI)
    e2 = nn(mt_t, s_mat, HI)
    tail = jnp.concatenate([t_t, -mt_t], axis=1)
    proj_ref[:BS, :BS] = theta
    proj_ref[BS:, :BS] = nn(t_t, s_mat - cross, HI)
    fence()
    wait_bytes(b_res.at[pl.ds(0, 7)], sems_b[2])
    fence()
    spun = nn(t_t, b_res[...].reshape(BS, 2 * BS) * inverse, HI)
    xq = spun[:, :BS] - e1
    qq = nt(jnp.concatenate([spun[:, BS:] - e2, xq], axis=1), tail, HI)
    proj_ref[:BS, BS:] = xq.T
    proj_ref[BS:, BS:] = qq.T
    proj_copy = pltpu.make_async_copy(proj_ref, proj_hbm, local_sem.at[4])
    proj_copy.start()
    assert counter[0] <= N_SEM
    fence()
    whole = w_ref.at[pl.ds(0, sent[0] // BLOCK_BYTES)]
    assert sent[0] % BLOCK_BYTES == 0
    remote(whole, whole, sibling, 0).wait_send()
    search_copy.wait()
    proj_copy.wait()


def shards(iterate, blocks, block_row, block_col, block_count):
    shape = jax.ShapeDtypeStruct
    rows1 = HALF + DEG
    node_total = iterate.shape[0] * lax.axis_size("rows") * lax.axis_size("cols")

    def buf(*dims, dtype=F32):
        return pltpu.VMEM(dims, dtype)

    def kernel(*refs):
        step_kernel(1.0 / node_total, *refs)

    outs = (shape(iterate.shape, BF16), shape((2 * BS, 2 * BS), F32))
    hbm = pl.BlockSpec(memory_space=pl.ANY)
    search, projected = pl.pallas_call(
        kernel,
        out_shape=outs,
        in_specs=[hbm, hbm, hbm, hbm, pl.BlockSpec(memory_space=pltpu.SMEM)],
        out_specs=(hbm, hbm),
        scratch_shapes=[
            buf(4 * BS, BS, dtype=BF16), buf(1, SLOTS, dtype=jnp.int32), buf(1, SLOTS, dtype=jnp.int32),
            buf(4 * BS, BS, dtype=BF16), buf(2 * BS, 2 * BS),
            buf(SLOTS + 1, BS, BS, dtype=BF16),
            buf(64, HALF, BS, dtype=BF16), buf(64, HALF, BS, dtype=BF16),
            buf(64, HALF, BS, dtype=BF16), buf(64, HALF, BS, dtype=BF16),
            buf(2, PAIRS, rows1, BS), buf(4, BS, BS), buf(8, 512, dtype=jnp.int32), buf(8, 512),
            pltpu.SMEM((8, 512), jnp.int32), pltpu.SMEM((8, 512), F32),
            buf(4, 4, rows1, BS), buf(4, 4, rows1, BS), buf(4, 4, HALF, BS), buf(4, 4, HALF, BS),
            buf(2, 3, 4, HALF, BS, dtype=BF16), buf(2, 3, 4, HALF, BS, dtype=BF16),
            buf(2, 3, 4, HALF, BS, dtype=BF16), buf(2, 3, 4, HALF, BS, dtype=BF16),
            buf(3, 4, DEG, BS), buf(3, 4, DEG, BS),
            buf(4, BS, BS), buf(4, DEG, BS),
            buf(2, 4, 4, BS, BS, dtype=BF16), buf(2, 4, 4, BS, BS, dtype=BF16),
            buf(8, 3, 16, BS), buf(7, 3, 16, BS), buf(4, 3, 16, BS), buf(4, 3, 16, BS), buf(8, 3, 16, BS),
            buf(8, 16, 2 * BS), buf(7, 16, 2 * BS), buf(16, 16, 2 * BS), buf(8, 16, 2 * BS),
            buf(8, BS), pltpu.SemaphoreType.DMA((1,)), pltpu.SemaphoreType.DMA((N_SEM,)), pltpu.SemaphoreType.DMA((10,)),
        ],
        compiler_params=pltpu.CompilerParams(
            collective_id=0, has_side_effects=True, vmem_limit_bytes=60 * 1024 * 1024),
        name="lobpcg_step",
    )(iterate, blocks.reshape(SLOTS, BS, BS), block_row.reshape(1, SLOTS), block_col.reshape(1, SLOTS),
      block_count.reshape(1, 1))

    def hand_over(search_ref, projected_ref, search_out, projected_out, search_v, projected_v, sems):
        pairs = [(search_ref, search_v, search_out), (projected_ref, projected_v, projected_out)]
        reads = [pltpu.make_async_copy(src, mid, sems.at[n]) for n, (src, mid, dst) in enumerate(pairs)]
        writes = [pltpu.make_async_copy(mid, dst, sems.at[n + 2]) for n, (src, mid, dst) in enumerate(pairs)]
        for copy in reads:
            copy.start()
        for n in range(2):
            reads[n].wait()
            writes[n].start()
        for copy in writes:
            copy.wait()

    return pl.pallas_call(
        hand_over, out_shape=outs, in_specs=[hbm, hbm], out_specs=(hbm, hbm),
        scratch_shapes=[buf(4 * BS, BS, dtype=BF16), buf(2 * BS, 2 * BS), pltpu.SemaphoreType.DMA((4,))],
        name="hand_over",
    )(search, projected)


def solution(mesh):
    placed = (
        P(("rows", "cols"), None),
        P("rows", "cols", None, None, None),
        P("rows", "cols", None),
        P("rows", "cols", None),
        P("rows", "cols"),
    )
    return jax.shard_map(
        shards,
        mesh=mesh,
        in_specs=placed,
        out_specs=(P(("rows", "cols"), None), P()),
        check_vma=False,
    )
```

```python
import math

import jax
import jax.numpy as jnp
from jax import lax
from jax.experimental import pallas as pl
from jax.experimental.pallas import tpu as pltpu
from jax.sharding import PartitionSpec as P

BS = 128
NY = 4
NZ = 4
NX = 4
NCOL = 8
GROUP = 32
SLOTS = 384
PAIRS = (SLOTS + GROUP) // 2
UNROLL = 52
PART = 96
DEG = 8
N_SEM = 120
HALF = BS // 2
BLOCK_BYTES = BS * BS * 2

F32 = jnp.float32
BF16 = jnp.bfloat16
HI = lax.Precision.HIGHEST


def nt(a, b, precision=None):
    return lax.dot_general(a, b, (((1,), (1,)), ((), ())), precision=precision, preferred_element_type=F32)


def nn(a, b, precision=None):
    return jnp.dot(a, b, precision=precision, preferred_element_type=F32)


def iota(shape, dim):
    return lax.broadcasted_iota(jnp.int32, shape, dim)


def flag(mask):
    return jnp.where(mask, 1.0, 0.0).astype(F32)


def sort_slots(row, col, count, a):
    live = iota((1, SLOTS), 1) < count
    local = jnp.where(live, row - a * GROUP, 2 * GROUP - 1)
    owner = col >> 5
    part = col & 3
    oy, oz = owner >> 2, owner & 3
    piece = part >> 1
    place = jnp.where(piece == 0, oz * 4 + oy, oy * 4 + oz)
    tile = piece * 32 + place * 2 + (part & 1)
    local_f = local.astype(F32)
    row_t = jnp.broadcast_to(local_f, (BS, SLOTS)).T
    lane = iota((SLOTS, BS), 1).astype(F32)
    hits = flag(row_t == lane)
    counts = jnp.sum(hits, axis=0, keepdims=True)
    counts = jnp.where(iota((1, BS), 1) < GROUP, counts, 0.0)
    pairs = ((counts.astype(jnp.int32) + 1) >> 1).astype(F32)
    upper = flag(iota((BS, BS), 0) < iota((BS, BS), 1)).astype(BF16)
    start = nn(jnp.broadcast_to(pairs, (16, BS)).astype(BF16), upper)[:1]
    row_w = jnp.concatenate([row_t] * (SLOTS // BS), axis=1)
    before = (row_w == local_f) & (iota((SLOTS, SLOTS), 1) < iota((SLOTS, SLOTS), 0))
    within = jnp.sum(flag(before), axis=1, keepdims=True)
    base = jnp.sum(hits * start, axis=1, keepdims=True)
    pos = 2.0 * base + within
    pos = jnp.where(row_t[:, :1] < GROUP, pos, 4096.0)
    onehot = flag(pos == iota((SLOTS, 512), 1).astype(F32)).astype(BF16)
    slot = iota((1, SLOTS), 1)
    values = jnp.concatenate(
        [(slot >> 4).astype(F32), (slot & 15).astype(F32), tile.astype(F32), jnp.ones((1, SLOTS), F32),
         jnp.zeros((12, SLOTS), F32)], axis=0).astype(BF16)
    placed = nn(values, onehot)
    perm = placed[0:1] * 16.0 + placed[1:2] + SLOTS * (1.0 - placed[3:4])
    start_t = jnp.broadcast_to(start, (BS, BS)).T
    pairs_t = jnp.broadcast_to(pairs, (BS, BS)).T
    lane4 = iota((BS, 512), 1).astype(F32)
    first = jnp.sum(flag((start_t[:, :1] == lane4) & (pairs_t[:, :1] > 0.0)), axis=0, keepdims=True)
    pad = jnp.zeros((1, 512 - BS), F32)
    last = jnp.concatenate([jnp.maximum(start + pairs - 1.0, 0.0), pad], axis=1)
    filled = jnp.concatenate([jnp.minimum(pairs, 1.0), pad], axis=1)
    ints = jnp.concatenate([perm, placed[2:3], last, jnp.zeros((5, 512), F32)], axis=0).astype(jnp.int32)
    floats = jnp.concatenate([1.0 - first, filled, jnp.zeros((6, 512), F32)], axis=0)
    return ints, floats


def half_inverse(block, midway=None):
    both = jnp.concatenate([block, flag(iota((HALF, HALF), 0) == iota((HALF, HALF), 1))], axis=1)
    rows = [both[8 * i:8 * i + 8] for i in range(8)]
    sub = iota((8, BS), 0)
    out = []

    def wide(v):
        return jnp.broadcast_to(v, (8, BS))

    for k in range(8):
        c = 8 * k
        lanes = [wide(rows[k][:, c + n:c + n + 1]) for n in range(8)]
        elem = [[wide(lanes[n][j:j + 1]) if n <= j else None for n in range(8)] for j in range(8)]
        inv = [[None] * 8 for unused in range(8)]
        roots, pivots = [], []
        for j in range(8):
            root = lax.rsqrt(elem[j][j])
            roots.append(root)
            pivots.append(root * root)
            mult = [elem[i][j] * pivots[j] if i > j else None for i in range(8)]
            for i in range(j + 1, 8):
                for n in range(j + 1, i + 1):
                    elem[i][n] = elem[i][n] - mult[i] * elem[n][j]
                for n in range(j):
                    inv[i][n] = inv[i][n] - mult[i] * inv[j][n]
                inv[i][j] = -mult[i]
        held = [wide(rows[k][j:j + 1]) for j in range(8)]
        first = []
        for j in range(8):
            total = held[j]
            for n in range(j):
                total = total + inv[j][n] * held[n]
            first.append(total)
        if k < 7:
            scaled = [first[j] * pivots[j] for j in range(8)]
            solved = []
            for j in range(8):
                total = scaled[j]
                for n in range(j + 1, 8):
                    total = total + inv[n][j] * scaled[n]
                solved.append(total)
            factors = [[wide(rows[i][:, c + j:c + j + 1]) for j in range(8)] for i in range(k + 1, 8)]
            for i in range(k + 1, 8):
                for j in range(8):
                    rows[i] = rows[i] - factors[i - k - 1][j] * solved[j]
        done = jnp.zeros((8, BS), F32)
        for j in range(8):
            done = jnp.where(sub == j, first[j] * roots[j], done)
        out.append(done)
        if k == 3 and midway is not None:
            midway()
    return jnp.concatenate(out, axis=0)[:, HALF:]


def step_kernel(inverse, x_hbm, w_hbm, row_hbm, col_hbm, cnt_ref, search_hbm, proj_hbm,
                x_ref, row_ref, col_ref, search_ref, proj_ref, w_ref,
                slab1a, slab1b, slab2a, slab2b, prod, xt_ref, ints_v, floats_v, ints_s, floats_s,
                siba_s, siba_r, sibb_s, sibb_r, hi_s, hi_r, lo_s, lo_r, deg_s, deg_r,
                lap_ref, deg_ref, x_group, l_group,
                a_part, a_r1, a_b2, a_b3, a_res, b_part, b_r1, b_b2, b_res,
                fence_ref, send_sem, recv_sem, local_sem):
    slab1, slab2 = (slab1a, slab1b), (slab2a, slab2b)
    sib_s, sib_r = (siba_s, sibb_s), (siba_r, sibb_r)
    a = lax.axis_index("rows")
    b = lax.axis_index("cols")
    y, z = a // NZ, a % NZ
    xx, core = b // 2, b % 2
    counter = [0]
    never = jnp.where(a >= NY * NZ, 1, 0)

    def fence():
        def body(unused, carry):
            fence_ref[...] = jnp.zeros_like(fence_ref)
            return carry

        lax.fori_loop(0, never, body, 0)


    def ydev(d):
        return {"rows": ((y + d + NY) % NY) * NZ + z, "cols": b}

    def zdev(d):
        return {"rows": y * NZ + (z + d + NZ) % NZ, "cols": b}

    def yzdev(d):
        return {"rows": ((y + d // NZ) % NY) * NZ + (z + d % NZ) % NZ, "cols": b}

    def coldev(d):
        return {"rows": a, "cols": (b + d) % NCOL}

    def xdev(d):
        return {"rows": a, "cols": ((xx + d) % NX) * 2 + core}

    sibling = {"rows": a, "cols": xx * 2 + (1 - core)}
    sent = [0]

    def new_sem():
        counter[0] += 1
        return counter[0] - 1

    def remote(src, dst, device, k):
        return pltpu.make_async_remote_copy(
            src_ref=src, dst_ref=dst, send_sem=send_sem.at[0], recv_sem=recv_sem.at[k],
            device_id=device, device_id_type=pl.DeviceIdType.MESH)

    def send(src, dst, device, k=None):
        copy = remote(src, dst, device, new_sem() if k is None else k)
        copy.start()
        sent[0] += math.prod(src.shape) * src.dtype.itemsize
        return copy

    def wait_bytes(like, k):
        remote(like, like, sibling, k).wait_recv()

    x_copy = pltpu.make_async_copy(x_hbm, x_ref, local_sem.at[3])
    x_copy.start()
    barrier = pltpu.get_barrier_semaphore()
    partners = [coldev(d) for d in range(1, NCOL)] + [yzdev(d) for d in range(1, NY * NZ)]
    for device in partners:
        pl.semaphore_signal(barrier, inc=1, device_id=device, device_id_type=pl.DeviceIdType.MESH)

    row_copy = pltpu.make_async_copy(row_hbm, row_ref, local_sem.at[4])
    col_copy = pltpu.make_async_copy(col_hbm, col_ref, local_sem.at[5])
    row_copy.start()
    col_copy.start()
    w_copies = [pltpu.make_async_copy(w_hbm.at[pl.ds(n * PART, PART)], w_ref.at[pl.ds(n * PART, PART)],
                                      local_sem.at[6 + n]) for n in range(SLOTS // PART)]
    for copy in w_copies:
        copy.start()
    x_copy.wait()

    place = ((z, y), (y, z))

    def span(p, i, j, size):
        return pl.ds(p * 32 + (i * 4 + j) * 2, size)

    for r in range(4):
        xt = x_ref[r * BS:(r + 1) * BS, :].astype(F32).T
        xt_ref[r] = xt
        xt = xt.astype(BF16)
        x_group[core, xx, r] = xt
        p, t = r // 2, r % 2
        for h in range(2):
            slab1[h][p * 32 + (place[p][0] * 4 + place[p][1]) * 2 + t] = xt[h * HALF:(h + 1) * HALF]
    w_ref[SLOTS] = jnp.zeros((BS, BS), BF16)
    fence()
    pl.semaphore_wait(barrier, len(partners))

    def gather(slab, direct):
        def first(p, d):
            return ydev(d) if p == 0 else zdev(d)

        def second(p, d):
            return zdev(d) if p == 0 else ydev(d)

        def block(p, i, j):
            return slab.at[span(p, i, j, 2)]

        def half(p, i, j, t):
            return slab.at[pl.ds(p * 32 + (i * 4 + j) * 2 + t, 1)]

        def spread(p, j):
            i = place[p][0]
            ref = block(p, i, j)
            return send(ref, ref, second(p, 1)), send(ref, ref, second(p, -1))

        def pass_on(p, j, pair, k):
            i = place[p][0]
            pair[0].wait_recv()
            one = half(p, (i + 3) % 4, j, 0)
            send(one, one, second(p, 1), k)
            pair[1].wait_recv()
            two = half(p, (i + 1) % 4, j, 1)
            send(two, two, second(p, -1), k)

        def spread_all(p, j):
            ref = block(p, place[p][0], j)
            for d in (2, 1, -1):
                send(ref, ref, second(p, d), ends)

        near, own, side, far = [], [], [], []
        ends = new_sem()
        for p in range(2):
            i, j = place[p]
            ref = block(p, i, j)
            near.append((send(ref, ref, first(p, 1)), send(ref, ref, first(p, -1))))
        for p in range(2):
            i, j = place[p]
            ref = block(p, i, j)
            far.append(send(ref, ref, first(p, 2)))
        if direct:
            for p in range(2):
                spread_all(p, place[p][1])
            yield
            for p in range(2):
                for n, j in enumerate((3, 1)):
                    near[p][n].wait_recv()
                    spread_all(p, (place[p][1] + j) % 4)
            yield
            for p in range(2):
                far[p].wait_recv()
                spread_all(p, (place[p][1] + 2) % 4)
            yield
            wait_bytes(slab.at[pl.ds(0, 48)], ends)
            yield
            return
        for p in range(2):
            own.append(spread(p, place[p][1]))
        yield
        for p in range(2):
            j = place[p][1]
            near[p][0].wait_recv()
            one = spread(p, (j + 3) % 4)
            near[p][1].wait_recv()
            side.append((one, spread(p, (j + 1) % 4)))
        yield
        for p in range(2):
            far[p].wait_recv()
            spread_all(p, (place[p][1] + 2) % 4)
        yield
        for p in range(2):
            pass_on(p, place[p][1], own[p], ends)
        yield
        for p in range(2):
            pass_on(p, (place[p][1] + 3) % 4, side[p][0], ends)
            pass_on(p, (place[p][1] + 1) % 4, side[p][1], ends)
        yield
        wait_bytes(slab.at[pl.ds(0, 24)], ends)
        yield

    def group_gather(buf):
        copies = [send(buf.at[core, xx], buf.at[core, xx], xdev(d)) for d in (2, 1, 3)]
        yield
        for copy in copies:
            copy.wait_recv()
        copy = send(buf.at[core], buf.at[core], sibling)
        yield
        copy.wait_recv()
        yield

    fence()
    g1 = [gather(slab1[h], False) for h in range(2)]
    next(g1[0])
    next(g1[1])
    xg = group_gather(x_group)
    next(xg)
    fence()
    row_copy.wait()
    col_copy.wait()
    ints, floats = sort_slots(row_ref[...], col_ref[...], cnt_ref[0, 0], a)
    ints_v[...] = ints
    floats_v[...] = floats
    ints_copy = pltpu.make_async_copy(ints_v, ints_s, local_sem.at[1])
    floats_copy = pltpu.make_async_copy(floats_v, floats_s, local_sem.at[2])
    ints_copy.start()
    floats_copy.start()
    def flip(n):
        def body(s, carry):
            w_ref[s] = w_ref[s].T
            return carry

        w_copies[n].wait()
        lax.fori_loop(n * PART, (n + 1) * PART, body, 0, unroll=16)

    fence()
    flip(0)
    fence()
    next(g1[0])
    fence()
    flip(1)
    fence()
    next(g1[0])
    fence()
    next(g1[0])
    fence()
    flip(2)
    fence()
    next(g1[0])
    fence()
    next(g1[1])
    fence()
    flip(3)
    fence()
    next(g1[1])
    next(xg)
    fence()
    ints_copy.wait()
    floats_copy.wait()
    xx_mat = sum(nt(xt_ref[r].astype(BF16), xt_ref[r].astype(BF16)) for r in range(4))
    a_part[:, 0] = xx_mat.reshape(8, 16, BS)
    fence()
    next(g1[0])

    def pick(kind, at, top):
        return jnp.clip(ints_s[kind, at], 0, top)

    def product(slab, h, with_degree, hooks):
        rows = HALF + DEG if with_degree else HALF
        ones = jnp.ones((16, 2 * BS), BF16)

        def body(n, acc):
            for u in range(UNROLL):
                s = n * UNROLL + u
                left = jnp.concatenate([slab[pick(1, 2 * s, 63)], slab[pick(1, 2 * s + 1, 63)]], axis=1)
                if with_degree:
                    left = jnp.concatenate([left, ones], axis=0)
                right = jnp.concatenate([w_ref[pick(0, 2 * s, SLOTS)], w_ref[pick(0, 2 * s + 1, SLOTS)]], axis=0)
                acc = acc * floats_s[0, s] + nn(left, right)[:rows]
                prod[h, s, :rows] = acc
            return acc

        acc = jnp.zeros((rows, BS), F32)
        at = 0
        for step, hook in hooks + [(PAIRS // UNROLL, None)]:
            acc = lax.fori_loop(at, step, body, acc)
            at = step
            if hook is not None:
                hook()

    def tile(h, g, rows):
        return prod[h, pick(2, g, PAIRS - 1), :rows] * floats_s[1, g]

    def order(d):
        return (xx + d) % NX

    def joined(ref):
        return jnp.concatenate([ref[r] for r in range(4)], axis=1)

    def halves(h):
        return pl.ds(h * HALF, HALF)

    from_sib, hi_copy, deg_copy, lo_copy = {}, {}, {}, {}

    def reduce_start(h):
        rows = HALF + DEG if h == 0 else HALF
        for d in (2, 1, 3, 0):
            for r in range(4):
                sib_s[h][d, r] = tile(h, (order(d) * 2 + (1 - core)) * 4 + r, rows)
            from_sib[h, d] = send(sib_s[h].at[d], sib_r[h].at[d], sibling)

    def reduce_middle(h):
        rows = HALF + DEG if h == 0 else HALF
        for d in (2, 1, 3, 0):
            from_sib[h, d].wait_recv()
            for r in range(4):
                total = tile(h, (order(d) * 2 + core) * 4 + r, rows) + sib_r[h][d, r]
                if d:
                    high = total[:HALF].astype(BF16)
                    hi_s[h, d - 1, r] = high
                    lo_s[h, d - 1, r] = (total[:HALF] - high.astype(F32)).astype(BF16)
                    if h == 0:
                        deg_s[d - 1, r] = total[HALF:]
                else:
                    lap_ref[r, halves(h)] = total[:HALF]
                    if h == 0:
                        deg_ref[r] = total[HALF:]
            if d:
                if h == 0:
                    deg_copy[d] = send(deg_s.at[d - 1], deg_r.at[d - 1], xdev(d))
                hi_copy[h, d] = send(hi_s.at[h, d - 1], hi_r.at[h, d - 1], xdev(d))

    def reduce_end(h):
        for d in (1, 3, 2):
            if h == 0:
                deg_copy[d].wait_recv()
            hi_copy[h, d].wait_recv()
        for r in range(4):
            if h == 0:
                deg_ref[r] = deg_ref[r] + deg_r[0, r] + deg_r[1, r] + deg_r[2, r]
            degree = jnp.broadcast_to(deg_ref[r][:1], (HALF, BS))
            summed = lap_ref[r, halves(h)] + sum(hi_r[h, d, r].astype(F32) for d in range(3))
            lap = degree * xt_ref[r, halves(h)] - summed
            lap_ref[r, halves(h)] = lap
            lap = lap.astype(BF16)
            l_group[core, xx, r, halves(h)] = lap
            p, t = r // 2, r % 2
            slab2[h][p * 32 + (place[p][0] * 4 + place[p][1]) * 2 + t] = lap

    def all_reduce(part, r1, b2, b3, res):
        sems = [new_sem() for unused in range(4)]
        for d in range(1, NCOL):
            send(part.at[(b + d) % NCOL], r1.at[d - 1], coldev(d), sems[0])
        yield
        wait_bytes(r1, sems[0])
        total = part[b]
        for d in range(1, NCOL):
            total = total + r1[d - 1]
        b2[y] = total
        for d in (1, 2, 3):
            send(b2.at[y], b2.at[y], ydev(d), sems[1])
        yield
        wait_bytes(b2.at[pl.ds(0, 3)], sems[1])
        b3[z] = b2[0] + b2[1] + b2[2] + b2[3]
        for d in (1, 2, 3):
            send(b3.at[z], b3.at[z], zdev(d), sems[2])
        yield
        wait_bytes(b3.at[pl.ds(0, 3)], sems[2])
        res[b] = b3[0] + b3[1] + b3[2] + b3[3]
        for d in range(1, NCOL):
            send(res.at[b], res.at[b], coldev(d), sems[3])
        yield
        wait_bytes(res.at[pl.ds(0, 7)], sems[3])
        yield

    fence()
    product(slab1[0], 0, True, [(1, lambda: (next(g1[1]), next(g1[1])))])
    fence()
    reduce_start(0)
    fence()
    next(g1[1])

    fence()
    product(slab1[1], 1, False, [(1, lambda: reduce_middle(0))])
    fence()
    reduce_start(1)
    fence()
    reduce_end(0)
    fence()
    g2 = [gather(slab2[h], False) for h in range(2)]
    next(g2[0])
    fence()
    reduce_middle(1)
    fence()
    next(g2[0])
    fence()
    next(g2[0])
    fence()
    next(g2[0])
    fence()
    reduce_end(1)
    fence()
    next(g2[1])
    fence()
    lap_all = joined(lap_ref)
    a_part[:, 1] = nt(joined(xt_ref), lap_all, HI).reshape(8, 16, BS)
    a_part[:, 2] = nt(lap_all, lap_all, HI).reshape(8, 16, BS)
    reduce_a = all_reduce(a_part, a_r1, a_b2, a_b3, a_res)
    next(reduce_a)
    lg = group_gather(l_group)
    next(lg)
    fence()
    next(g2[0])
    fence()
    next(g2[1])
    fence()
    next(g2[1])
    fence()
    scaled = joined(lap_ref) * jnp.concatenate([jnp.broadcast_to(deg_ref[r][:1], (BS, BS)) for r in range(4)], axis=1)
    pair_rows = jnp.concatenate([joined(xt_ref), joined(lap_ref)], axis=0)
    b_part[...] = nt(scaled, pair_rows, HI).reshape(8, 16, 2 * BS)
    fence()
    next(reduce_a)
    fence()
    next(g2[0])

    def early():
        next(g2[1])
        next(g2[1])
        for h in range(2):
            for d in (2, 1, 3):
                lo_copy[h, d] = send(lo_s.at[h, d - 1], lo_r.at[h, d - 1], xdev(d))

    fence()
    product(slab2[0], 0, False, [(1, early)])
    fence()
    next(lg)
    fence()
    next(g2[1])
    fence()
    product(slab2[1], 1, False, [(1, lambda: next(reduce_a))])
    fence()
    next(lg)
    next(xg)
    fence()
    total = jnp.zeros((BS, 2 * BS), F32)
    for c in range(2):
        for k in range(4):
            for r in (0, 2):
                g = (k * 2 + c) * 4 + r
                part = jnp.concatenate(
                    [jnp.concatenate([tile(h, g, HALF), tile(h, g + 1, HALF)], axis=1) for h in range(2)], axis=0)
                top = jnp.concatenate([x_group[c, k, r], x_group[c, k, r + 1]], axis=1)
                low = jnp.concatenate([l_group[c, k, r], l_group[c, k, r + 1]], axis=1)
                total = total + nt(part.astype(BF16), jnp.concatenate([top, low], axis=0))
    b_part[...] = b_part[...] - total.reshape(8, 16, 2 * BS)
    fence()
    sems_b = [new_sem() for unused in range(3)]
    for d in range(1, NCOL):
        send(b_part.at[(b + d) % NCOL], b_r1.at[d - 1], coldev(d), sems_b[0])
    fence()
    next(reduce_a)
    fence()
    wait_bytes(b_r1, sems_b[0])
    part = b_part[b]
    for d in range(1, NCOL):
        part = part + b_r1[d - 1]
    b_b2[a] = part
    for d in range(1, NY * NZ):
        send(b_b2.at[a], b_b2.at[a], yzdev(d), sems_b[1])
    fence()
    next(reduce_a)
    fence()
    def mat(m):
        return a_res[:, m].reshape(BS, BS) * inverse

    gx, theta, s_mat = mat(0), mat(1), mat(2)
    m = 2.0 * theta - nn(gx, theta, HI)
    m_t = m.T
    cross = nn(m_t, theta, HI)
    gram = s_mat - cross.T - cross + nn(m_t, nn(gx, m, HI), HI)
    fence()
    inv_a = half_inverse(gram[:HALF, :HALF])
    side = nt(gram[HALF:, :HALF], inv_a, HI)
    def gathered():
        fence()
        wait_bytes(b_b2.at[pl.ds(0, NY * NZ - 1)], sems_b[1])
        part = b_b2[0]
        for k in range(1, NY * NZ):
            part = part + b_b2[k]
        b_res[b] = part
        for d in range(1, NCOL):
            send(b_res.at[b], b_res.at[b], coldev(d), sems_b[2])
        fence()

    fence()
    inv_c = half_inverse(gram[HALF:, HALF:] - nt(side, side, HI), gathered)
    corner = nn(inv_c, nn(side, inv_a, HI), HI)
    t_t = jnp.concatenate(
        [jnp.concatenate([inv_a, jnp.zeros((HALF, HALF), F32)], axis=1), jnp.concatenate([-corner, inv_c], axis=1)],
        axis=0)
    fence()
    for h in range(2):
        for d in (1, 3, 2):
            lo_copy[h, d].wait_recv()
    fence()
    mt_t = nt(t_t, m, HI)
    for r in range(4):
        low = [sum(lo_r[h, d, r].astype(F32) for d in range(3)) for h in range(2)]
        lap = lap_ref[r] - jnp.concatenate(low, axis=0)
        part = nn(t_t, lap, HI) - nn(mt_t, xt_ref[r], HI)
        search_ref[r * BS:(r + 1) * BS, :] = part.T.astype(BF16)
    search_copy = pltpu.make_async_copy(search_ref, search_hbm, local_sem.at[3])
    search_copy.start()
    e1 = nt(mt_t, theta, HI)
    e2 = nn(mt_t, s_mat, HI)
    tail = jnp.concatenate([t_t, -mt_t], axis=1)
    proj_ref[:BS, :BS] = theta
    proj_ref[BS:, :BS] = nn(t_t, s_mat - cross, HI)
    fence()
    wait_bytes(b_res.at[pl.ds(0, 7)], sems_b[2])
    fence()
    spun = nn(t_t, b_res[...].reshape(BS, 2 * BS) * inverse, HI)
    xq = spun[:, :BS] - e1
    qq = nt(jnp.concatenate([spun[:, BS:] - e2, xq], axis=1), tail, HI)
    proj_ref[:BS, BS:] = xq.T
    proj_ref[BS:, BS:] = qq.T
    proj_copy = pltpu.make_async_copy(proj_ref, proj_hbm, local_sem.at[4])
    proj_copy.start()
    assert counter[0] <= N_SEM
    fence()
    whole = w_ref.at[pl.ds(0, sent[0] // BLOCK_BYTES)]
    assert sent[0] % BLOCK_BYTES == 0
    remote(whole, whole, sibling, 0).wait_send()
    search_copy.wait()
    proj_copy.wait()


def shards(iterate, blocks, block_row, block_col, block_count):
    shape = jax.ShapeDtypeStruct
    rows1 = HALF + DEG
    node_total = iterate.shape[0] * lax.axis_size("rows") * lax.axis_size("cols")

    def buf(*dims, dtype=F32):
        return pltpu.VMEM(dims, dtype)

    def kernel(*refs):
        step_kernel(1.0 / node_total, *refs)

    outs = (shape(iterate.shape, BF16), shape((2 * BS, 2 * BS), F32))
    hbm = pl.BlockSpec(memory_space=pl.ANY)
    search, projected = pl.pallas_call(
        kernel,
        out_shape=outs,
        in_specs=[hbm, hbm, hbm, hbm, pl.BlockSpec(memory_space=pltpu.SMEM)],
        out_specs=(hbm, hbm),
        scratch_shapes=[
            buf(4 * BS, BS, dtype=BF16), buf(1, SLOTS, dtype=jnp.int32), buf(1, SLOTS, dtype=jnp.int32),
            buf(4 * BS, BS, dtype=BF16), buf(2 * BS, 2 * BS),
            buf(SLOTS + 1, BS, BS, dtype=BF16),
            buf(64, HALF, BS, dtype=BF16), buf(64, HALF, BS, dtype=BF16),
            buf(64, HALF, BS, dtype=BF16), buf(64, HALF, BS, dtype=BF16),
            buf(2, PAIRS, rows1, BS), buf(4, BS, BS), buf(8, 512, dtype=jnp.int32), buf(8, 512),
            pltpu.SMEM((8, 512), jnp.int32), pltpu.SMEM((8, 512), F32),
            buf(4, 4, rows1, BS), buf(4, 4, rows1, BS), buf(4, 4, HALF, BS), buf(4, 4, HALF, BS),
            buf(2, 3, 4, HALF, BS, dtype=BF16), buf(2, 3, 4, HALF, BS, dtype=BF16),
            buf(2, 3, 4, HALF, BS, dtype=BF16), buf(2, 3, 4, HALF, BS, dtype=BF16),
            buf(3, 4, DEG, BS), buf(3, 4, DEG, BS),
            buf(4, BS, BS), buf(4, DEG, BS),
            buf(2, 4, 4, BS, BS, dtype=BF16), buf(2, 4, 4, BS, BS, dtype=BF16),
            buf(8, 3, 16, BS), buf(7, 3, 16, BS), buf(4, 3, 16, BS), buf(4, 3, 16, BS), buf(8, 3, 16, BS),
            buf(8, 16, 2 * BS), buf(7, 16, 2 * BS), buf(16, 16, 2 * BS), buf(8, 16, 2 * BS),
            buf(8, BS), pltpu.SemaphoreType.DMA((1,)), pltpu.SemaphoreType.DMA((N_SEM,)), pltpu.SemaphoreType.DMA((10,)),
        ],
        compiler_params=pltpu.CompilerParams(
            collective_id=0, has_side_effects=True, vmem_limit_bytes=60 * 1024 * 1024),
        name="lobpcg_step",
    )(iterate, blocks.reshape(SLOTS, BS, BS), block_row.reshape(1, SLOTS), block_col.reshape(1, SLOTS),
      block_count.reshape(1, 1))

    def hand_over(search_ref, projected_ref, search_out, projected_out, search_v, projected_v, sems):
        pairs = [(search_ref, search_v, search_out), (projected_ref, projected_v, projected_out)]
        reads = [pltpu.make_async_copy(src, mid, sems.at[n]) for n, (src, mid, dst) in enumerate(pairs)]
        writes = [pltpu.make_async_copy(mid, dst, sems.at[n + 2]) for n, (src, mid, dst) in enumerate(pairs)]
        for copy in reads:
            copy.start()
        for n in range(2):
            reads[n].wait()
            writes[n].start()
        for copy in writes:
            copy.wait()

    return pl.pallas_call(
        hand_over, out_shape=outs, in_specs=[hbm, hbm], out_specs=(hbm, hbm),
        scratch_shapes=[buf(4 * BS, BS, dtype=BF16), buf(2 * BS, 2 * BS), pltpu.SemaphoreType.DMA((4,))],
        name="hand_over",
    )(search, projected)


def solution(mesh):
    placed = (
        P(("rows", "cols"), None),
        P("rows", "cols", None, None, None),
        P("rows", "cols", None),
        P("rows", "cols", None),
        P("rows", "cols"),
    )
    return jax.shard_map(
        shards,
        mesh=mesh,
        in_specs=placed,
        out_specs=(P(("rows", "cols"), None), P()),
        check_vma=False,
    )
```

```python
import math

import jax
import jax.numpy as jnp
from jax import lax
from jax.experimental import pallas as pl
from jax.experimental.pallas import tpu as pltpu
from jax.sharding import PartitionSpec as P

BS = 128
NY = 4
NZ = 4
NX = 4
NCOL = 8
GROUP = 32
SLOTS = 384
PAIRS = (SLOTS + GROUP) // 2
UNROLL = 52
PART = 96
DEG = 8
N_SEM = 120
HALF = BS // 2
BLOCK_BYTES = BS * BS * 2

F32 = jnp.float32
BF16 = jnp.bfloat16
HI = lax.Precision.HIGHEST


def nt(a, b, precision=None):
    return lax.dot_general(a, b, (((1,), (1,)), ((), ())), precision=precision, preferred_element_type=F32)


def nn(a, b, precision=None):
    return jnp.dot(a, b, precision=precision, preferred_element_type=F32)


def iota(shape, dim):
    return lax.broadcasted_iota(jnp.int32, shape, dim)


def flag(mask):
    return jnp.where(mask, 1.0, 0.0).astype(F32)


def sort_slots(row, col, count, a):
    live = iota((1, SLOTS), 1) < count
    local = jnp.where(live, row - a * GROUP, 2 * GROUP - 1)
    owner = col >> 5
    part = col & 3
    oy, oz = owner >> 2, owner & 3
    piece = part >> 1
    place = jnp.where(piece == 0, oz * 4 + oy, oy * 4 + oz)
    tile = piece * 32 + place * 2 + (part & 1)
    local_f = local.astype(F32)
    row_t = jnp.broadcast_to(local_f, (BS, SLOTS)).T
    lane = iota((SLOTS, BS), 1).astype(F32)
    hits = flag(row_t == lane)
    counts = jnp.sum(hits, axis=0, keepdims=True)
    counts = jnp.where(iota((1, BS), 1) < GROUP, counts, 0.0)
    pairs = ((counts.astype(jnp.int32) + 1) >> 1).astype(F32)
    upper = flag(iota((BS, BS), 0) < iota((BS, BS), 1)).astype(BF16)
    start = nn(jnp.broadcast_to(pairs, (16, BS)).astype(BF16), upper)[:1]
    row_w = jnp.concatenate([row_t] * (SLOTS // BS), axis=1)
    before = (row_w == local_f) & (iota((SLOTS, SLOTS), 1) < iota((SLOTS, SLOTS), 0))
    within = jnp.sum(flag(before), axis=1, keepdims=True)
    base = jnp.sum(hits * start, axis=1, keepdims=True)
    pos = 2.0 * base + within
    pos = jnp.where(row_t[:, :1] < GROUP, pos, 4096.0)
    onehot = flag(pos == iota((SLOTS, 512), 1).astype(F32)).astype(BF16)
    slot = iota((1, SLOTS), 1)
    values = jnp.concatenate(
        [(slot >> 4).astype(F32), (slot & 15).astype(F32), tile.astype(F32), jnp.ones((1, SLOTS), F32),
         jnp.zeros((12, SLOTS), F32)], axis=0).astype(BF16)
    placed = nn(values, onehot)
    perm = placed[0:1] * 16.0 + placed[1:2] + SLOTS * (1.0 - placed[3:4])
    start_t = jnp.broadcast_to(start, (BS, BS)).T
    pairs_t = jnp.broadcast_to(pairs, (BS, BS)).T
    lane4 = iota((BS, 512), 1).astype(F32)
    first = jnp.sum(flag((start_t[:, :1] == lane4) & (pairs_t[:, :1] > 0.0)), axis=0, keepdims=True)
    pad = jnp.zeros((1, 512 - BS), F32)
    last = jnp.concatenate([jnp.maximum(start + pairs - 1.0, 0.0), pad], axis=1)
    filled = jnp.concatenate([jnp.minimum(pairs, 1.0), pad], axis=1)
    ints = jnp.concatenate([perm, placed[2:3], last, jnp.zeros((5, 512), F32)], axis=0).astype(jnp.int32)
    floats = jnp.concatenate([1.0 - first, filled, jnp.zeros((6, 512), F32)], axis=0)
    return ints, floats


def half_inverse(block, midway=None):
    both = jnp.concatenate([block, flag(iota((HALF, HALF), 0) == iota((HALF, HALF), 1))], axis=1)
    rows = [both[8 * i:8 * i + 8] for i in range(8)]
    sub = iota((8, BS), 0)
    out = []

    def wide(v):
        return jnp.broadcast_to(v, (8, BS))

    for k in range(8):
        c = 8 * k
        lanes = [wide(rows[k][:, c + n:c + n + 1]) for n in range(8)]
        elem = [[wide(lanes[n][j:j + 1]) if n <= j else None for n in range(8)] for j in range(8)]
        inv = [[None] * 8 for unused in range(8)]
        roots, pivots = [], []
        for j in range(8):
            root = lax.rsqrt(elem[j][j])
            roots.append(root)
            pivots.append(root * root)
            mult = [elem[i][j] * pivots[j] if i > j else None for i in range(8)]
            for i in range(j + 1, 8):
                for n in range(j + 1, i + 1):
                    elem[i][n] = elem[i][n] - mult[i] * elem[n][j]
                for n in range(j):
                    inv[i][n] = inv[i][n] - mult[i] * inv[j][n]
                inv[i][j] = -mult[i]
        held = [wide(rows[k][j:j + 1]) for j in range(8)]
        first = []
        for j in range(8):
            total = held[j]
            for n in range(j):
                total = total + inv[j][n] * held[n]
            first.append(total)
        if k < 7:
            scaled = [first[j] * pivots[j] for j in range(8)]
            solved = []
            for j in range(8):
                total = scaled[j]
                for n in range(j + 1, 8):
                    total = total + inv[n][j] * scaled[n]
                solved.append(total)
            factors = [[wide(rows[i][:, c + j:c + j + 1]) for j in range(8)] for i in range(k + 1, 8)]
            for i in range(k + 1, 8):
                for j in range(8):
                    rows[i] = rows[i] - factors[i - k - 1][j] * solved[j]
        done = jnp.zeros((8, BS), F32)
        for j in range(8):
            done = jnp.where(sub == j, first[j] * roots[j], done)
        out.append(done)
        if k == 3 and midway is not None:
            midway()
    return jnp.concatenate(out, axis=0)[:, HALF:]


def step_kernel(inverse, x_hbm, w_hbm, row_hbm, col_hbm, cnt_ref, search_hbm, proj_hbm,
                x_ref, row_ref, col_ref, search_ref, proj_ref, w_ref,
                slab1a, slab1b, slab2a, slab2b, prod, xt_ref, ints_v, floats_v, ints_s, floats_s,
                siba_s, siba_r, sibb_s, sibb_r, hi_s, hi_r, lo_s, lo_r, deg_s, deg_r,
                lap_ref, deg_ref, x_group, l_group,
                a_part, a_r1, a_b2, a_b3, a_res, b_part, b_r1, b_b2, b_res,
                fence_ref, send_sem, recv_sem, local_sem):
    slab1, slab2 = (slab1a, slab1b), (slab2a, slab2b)
    sib_s, sib_r = (siba_s, sibb_s), (siba_r, sibb_r)
    a = lax.axis_index("rows")
    b = lax.axis_index("cols")
    y, z = a // NZ, a % NZ
    xx, core = b // 2, b % 2
    counter = [0]
    never = jnp.where(a >= NY * NZ, 1, 0)

    def fence():
        def body(unused, carry):
            fence_ref[...] = jnp.zeros_like(fence_ref)
            return carry

        lax.fori_loop(0, never, body, 0)


    def ydev(d):
        return {"rows": ((y + d + NY) % NY) * NZ + z, "cols": b}

    def zdev(d):
        return {"rows": y * NZ + (z + d + NZ) % NZ, "cols": b}

    def yzdev(d):
        return {"rows": ((y + d // NZ) % NY) * NZ + (z + d % NZ) % NZ, "cols": b}

    def coldev(d):
        return {"rows": a, "cols": (b + d) % NCOL}

    def xdev(d):
        return {"rows": a, "cols": ((xx + d) % NX) * 2 + core}

    sibling = {"rows": a, "cols": xx * 2 + (1 - core)}
    sent = [0]

    def new_sem():
        counter[0] += 1
        return counter[0] - 1

    def remote(src, dst, device, k):
        return pltpu.make_async_remote_copy(
            src_ref=src, dst_ref=dst, send_sem=send_sem.at[0], recv_sem=recv_sem.at[k],
            device_id=device, device_id_type=pl.DeviceIdType.MESH)

    def send(src, dst, device, k=None):
        copy = remote(src, dst, device, new_sem() if k is None else k)
        copy.start()
        sent[0] += math.prod(src.shape) * src.dtype.itemsize
        return copy

    def wait_bytes(like, k):
        remote(like, like, sibling, k).wait_recv()

    x_copy = pltpu.make_async_copy(x_hbm, x_ref, local_sem.at[3])
    x_copy.start()
    barrier = pltpu.get_barrier_semaphore()
    partners = [coldev(d) for d in range(1, NCOL)] + [yzdev(d) for d in range(1, NY * NZ)]
    for device in partners:
        pl.semaphore_signal(barrier, inc=1, device_id=device, device_id_type=pl.DeviceIdType.MESH)

    row_copy = pltpu.make_async_copy(row_hbm, row_ref, local_sem.at[4])
    col_copy = pltpu.make_async_copy(col_hbm, col_ref, local_sem.at[5])
    row_copy.start()
    col_copy.start()
    w_copies = [pltpu.make_async_copy(w_hbm.at[pl.ds(n * PART, PART)], w_ref.at[pl.ds(n * PART, PART)],
                                      local_sem.at[6 + n]) for n in range(SLOTS // PART)]
    for copy in w_copies:
        copy.start()
    x_copy.wait()

    place = ((z, y), (y, z))

    def span(p, i, j, size):
        return pl.ds(p * 32 + (i * 4 + j) * 2, size)

    for r in range(4):
        xt = x_ref[r * BS:(r + 1) * BS, :].astype(F32).T
        xt_ref[r] = xt
        xt = xt.astype(BF16)
        x_group[core, xx, r] = xt
        p, t = r // 2, r % 2
        for h in range(2):
            slab1[h][p * 32 + (place[p][0] * 4 + place[p][1]) * 2 + t] = xt[h * HALF:(h + 1) * HALF]
    w_ref[SLOTS] = jnp.zeros((BS, BS), BF16)
    fence()
    pl.semaphore_wait(barrier, len(partners))

    def gather(slab, direct):
        def first(p, d):
            return ydev(d) if p == 0 else zdev(d)

        def second(p, d):
            return zdev(d) if p == 0 else ydev(d)

        def block(p, i, j):
            return slab.at[span(p, i, j, 2)]

        def half(p, i, j, t):
            return slab.at[pl.ds(p * 32 + (i * 4 + j) * 2 + t, 1)]

        def spread(p, j):
            i = place[p][0]
            ref = block(p, i, j)
            return send(ref, ref, second(p, 1)), send(ref, ref, second(p, -1))

        def pass_on(p, j, pair, k):
            i = place[p][0]
            pair[0].wait_recv()
            one = half(p, (i + 3) % 4, j, 0)
            send(one, one, second(p, 1), k)
            pair[1].wait_recv()
            two = half(p, (i + 1) % 4, j, 1)
            send(two, two, second(p, -1), k)

        def spread_all(p, j):
            ref = block(p, place[p][0], j)
            for d in (2, 1, -1):
                send(ref, ref, second(p, d), ends)

        near, own, side, far = [], [], [], []
        ends = new_sem()
        for p in range(2):
            i, j = place[p]
            ref = block(p, i, j)
            near.append((send(ref, ref, first(p, 1)), send(ref, ref, first(p, -1))))
        for p in range(2):
            i, j = place[p]
            ref = block(p, i, j)
            far.append(send(ref, ref, first(p, 2)))
        if direct:
            for p in range(2):
                spread_all(p, place[p][1])
            yield
            for p in range(2):
                for n, j in enumerate((3, 1)):
                    near[p][n].wait_recv()
                    spread_all(p, (place[p][1] + j) % 4)
            yield
            for p in range(2):
                far[p].wait_recv()
                spread_all(p, (place[p][1] + 2) % 4)
            yield
            wait_bytes(slab.at[pl.ds(0, 48)], ends)
            yield
            return
        for p in range(2):
            own.append(spread(p, place[p][1]))
        yield
        for p in range(2):
            j = place[p][1]
            near[p][0].wait_recv()
            one = spread(p, (j + 3) % 4)
            near[p][1].wait_recv()
            side.append((one, spread(p, (j + 1) % 4)))
        yield
        for p in range(2):
            far[p].wait_recv()
            spread_all(p, (place[p][1] + 2) % 4)
        yield
        for p in range(2):
            pass_on(p, place[p][1], own[p], ends)
        yield
        for p in range(2):
            pass_on(p, (place[p][1] + 3) % 4, side[p][0], ends)
            pass_on(p, (place[p][1] + 1) % 4, side[p][1], ends)
        yield
        wait_bytes(slab.at[pl.ds(0, 24)], ends)
        yield

    def group_gather(buf):
        copies = [send(buf.at[core, xx], buf.at[core, xx], xdev(d)) for d in (2, 1, 3)]
        yield
        for copy in copies:
            copy.wait_recv()
        copy = send(buf.at[core], buf.at[core], sibling)
        yield
        copy.wait_recv()
        yield

    fence()
    g1 = [gather(slab1[h], False) for h in range(2)]
    next(g1[0])
    next(g1[1])
    xg = group_gather(x_group)
    next(xg)
    fence()
    row_copy.wait()
    col_copy.wait()
    ints, floats = sort_slots(row_ref[...], col_ref[...], cnt_ref[0, 0], a)
    ints_v[...] = ints
    floats_v[...] = floats
    ints_copy = pltpu.make_async_copy(ints_v, ints_s, local_sem.at[1])
    floats_copy = pltpu.make_async_copy(floats_v, floats_s, local_sem.at[2])
    ints_copy.start()
    floats_copy.start()
    def flip(n):
        def body(s, carry):
            w_ref[s] = w_ref[s].T
            return carry

        w_copies[n].wait()
        lax.fori_loop(n * PART, (n + 1) * PART, body, 0, unroll=16)

    fence()
    flip(0)
    fence()
    next(g1[0])
    fence()
    flip(1)
    fence()
    next(g1[0])
    fence()
    next(g1[0])
    fence()
    flip(2)
    fence()
    next(g1[0])
    fence()
    next(g1[1])
    fence()
    flip(3)
    fence()
    next(g1[1])
    next(xg)
    fence()
    ints_copy.wait()
    floats_copy.wait()
    xx_mat = sum(nt(xt_ref[r].astype(BF16), xt_ref[r].astype(BF16)) for r in range(4))
    a_part[:, 0] = xx_mat.reshape(8, 16, BS)
    fence()
    next(g1[0])

    def pick(kind, at, top):
        return jnp.clip(ints_s[kind, at], 0, top)

    def product(slab, h, with_degree, hooks):
        rows = HALF + DEG if with_degree else HALF
        ones = jnp.ones((16, 2 * BS), BF16)

        def body(n, acc):
            for u in range(UNROLL):
                s = n * UNROLL + u
                left = jnp.concatenate([slab[pick(1, 2 * s, 63)], slab[pick(1, 2 * s + 1, 63)]], axis=1)
                if with_degree:
                    left = jnp.concatenate([left, ones], axis=0)
                right = jnp.concatenate([w_ref[pick(0, 2 * s, SLOTS)], w_ref[pick(0, 2 * s + 1, SLOTS)]], axis=0)
                acc = acc * floats_s[0, s] + nn(left, right)[:rows]
                prod[h, s, :rows] = acc
            return acc

        acc = jnp.zeros((rows, BS), F32)
        at = 0
        for step, hook in hooks + [(PAIRS // UNROLL, None)]:
            acc = lax.fori_loop(at, step, body, acc)
            at = step
            if hook is not None:
                hook()

    def tile(h, g, rows):
        return prod[h, pick(2, g, PAIRS - 1), :rows] * floats_s[1, g]

    def order(d):
        return (xx + d) % NX

    def joined(ref):
        return jnp.concatenate([ref[r] for r in range(4)], axis=1)

    def halves(h):
        return pl.ds(h * HALF, HALF)

    from_sib, hi_copy, deg_copy, lo_copy = {}, {}, {}, {}

    def reduce_start(h):
        rows = HALF + DEG if h == 0 else HALF
        for d in (2, 1, 3, 0):
            for r in range(4):
                sib_s[h][d, r] = tile(h, (order(d) * 2 + (1 - core)) * 4 + r, rows)
            from_sib[h, d] = send(sib_s[h].at[d], sib_r[h].at[d], sibling)

    def reduce_middle(h):
        rows = HALF + DEG if h == 0 else HALF
        for d in (2, 1, 3, 0):
            from_sib[h, d].wait_recv()
            for r in range(4):
                total = tile(h, (order(d) * 2 + core) * 4 + r, rows) + sib_r[h][d, r]
                if d:
                    high = total[:HALF].astype(BF16)
                    hi_s[h, d - 1, r] = high
                    lo_s[h, d - 1, r] = (total[:HALF] - high.astype(F32)).astype(BF16)
                    if h == 0:
                        deg_s[d - 1, r] = total[HALF:]
                else:
                    lap_ref[r, halves(h)] = total[:HALF]
                    if h == 0:
                        deg_ref[r] = total[HALF:]
            if d:
                if h == 0:
                    deg_copy[d] = send(deg_s.at[d - 1], deg_r.at[d - 1], xdev(d))
                hi_copy[h, d] = send(hi_s.at[h, d - 1], hi_r.at[h, d - 1], xdev(d))

    def reduce_end(h):
        for d in (1, 3, 2):
            if h == 0:
                deg_copy[d].wait_recv()
            hi_copy[h, d].wait_recv()
        for r in range(4):
            if h == 0:
                deg_ref[r] = deg_ref[r] + deg_r[0, r] + deg_r[1, r] + deg_r[2, r]
            degree = jnp.broadcast_to(deg_ref[r][:1], (HALF, BS))
            summed = lap_ref[r, halves(h)] + sum(hi_r[h, d, r].astype(F32) for d in range(3))
            lap = degree * xt_ref[r, halves(h)] - summed
            lap_ref[r, halves(h)] = lap
            lap = lap.astype(BF16)
            l_group[core, xx, r, halves(h)] = lap
            p, t = r // 2, r % 2
            slab2[h][p * 32 + (place[p][0] * 4 + place[p][1]) * 2 + t] = lap

    def all_reduce(part, r1, b2, b3, res):
        sems = [new_sem() for unused in range(4)]
        for d in range(1, NCOL):
            send(part.at[(b + d) % NCOL], r1.at[d - 1], coldev(d), sems[0])
        yield
        wait_bytes(r1, sems[0])
        total = part[b]
        for d in range(1, NCOL):
            total = total + r1[d - 1]
        b2[y] = total
        for d in (1, 2, 3):
            send(b2.at[y], b2.at[y], ydev(d), sems[1])
        yield
        wait_bytes(b2.at[pl.ds(0, 3)], sems[1])
        b3[z] = b2[0] + b2[1] + b2[2] + b2[3]
        for d in (1, 2, 3):
            send(b3.at[z], b3.at[z], zdev(d), sems[2])
        yield
        wait_bytes(b3.at[pl.ds(0, 3)], sems[2])
        res[b] = b3[0] + b3[1] + b3[2] + b3[3]
        for d in range(1, NCOL):
            send(res.at[b], res.at[b], coldev(d), sems[3])
        yield
        wait_bytes(res.at[pl.ds(0, 7)], sems[3])
        yield

    fence()
    product(slab1[0], 0, True, [(1, lambda: (next(g1[1]), next(g1[1])))])
    fence()
    reduce_start(0)
    fence()
    next(g1[1])

    fence()
    product(slab1[1], 1, False, [(1, lambda: reduce_middle(0))])
    fence()
    reduce_start(1)
    fence()
    reduce_end(0)
    fence()
    g2 = [gather(slab2[h], False) for h in range(2)]
    next(g2[0])
    fence()
    reduce_middle(1)
    fence()
    next(g2[0])
    fence()
    next(g2[0])
    fence()
    next(g2[0])
    fence()
    reduce_end(1)
    fence()
    next(g2[1])
    fence()
    lap_all = joined(lap_ref)
    a_part[:, 1] = nt(joined(xt_ref), lap_all, HI).reshape(8, 16, BS)
    a_part[:, 2] = nt(lap_all, lap_all, HI).reshape(8, 16, BS)
    reduce_a = all_reduce(a_part, a_r1, a_b2, a_b3, a_res)
    next(reduce_a)
    lg = group_gather(l_group)
    next(lg)
    fence()
    next(g2[0])
    fence()
    next(g2[1])
    fence()
    next(g2[1])
    fence()
    scaled = joined(lap_ref) * jnp.concatenate([jnp.broadcast_to(deg_ref[r][:1], (BS, BS)) for r in range(4)], axis=1)
    pair_rows = jnp.concatenate([joined(xt_ref), joined(lap_ref)], axis=0)
    b_part[...] = nt(scaled, pair_rows, HI).reshape(8, 16, 2 * BS)
    fence()
    next(reduce_a)
    fence()
    next(g2[0])

    def early():
        next(g2[1])
        next(g2[1])
        for h in range(2):
            for d in (2, 1, 3):
                lo_copy[h, d] = send(lo_s.at[h, d - 1], lo_r.at[h, d - 1], xdev(d))

    fence()
    product(slab2[0], 0, False, [(1, early)])
    fence()
    next(lg)
    fence()
    next(g2[1])
    fence()
    product(slab2[1], 1, False, [(1, lambda: next(reduce_a))])
    fence()
    next(lg)
    next(xg)
    fence()
    total = jnp.zeros((BS, 2 * BS), F32)
    for c in range(2):
        for k in range(4):
            for r in (0, 2):
                g = (k * 2 + c) * 4 + r
                part = jnp.concatenate(
                    [jnp.concatenate([tile(h, g, HALF), tile(h, g + 1, HALF)], axis=1) for h in range(2)], axis=0)
                top = jnp.concatenate([x_group[c, k, r], x_group[c, k, r + 1]], axis=1)
                low = jnp.concatenate([l_group[c, k, r], l_group[c, k, r + 1]], axis=1)
                total = total + nt(part.astype(BF16), jnp.concatenate([top, low], axis=0))
    b_part[...] = b_part[...] - total.reshape(8, 16, 2 * BS)
    fence()
    sems_b = [new_sem() for unused in range(3)]
    for d in range(1, NCOL):
        send(b_part.at[(b + d) % NCOL], b_r1.at[d - 1], coldev(d), sems_b[0])
    fence()
    next(reduce_a)
    fence()
    wait_bytes(b_r1, sems_b[0])
    part = b_part[b]
    for d in range(1, NCOL):
        part = part + b_r1[d - 1]
    b_b2[a] = part
    for d in range(1, NY * NZ):
        send(b_b2.at[a], b_b2.at[a], yzdev(d), sems_b[1])
    fence()
    next(reduce_a)
    fence()
    def mat(m):
        return a_res[:, m].reshape(BS, BS) * inverse

    gx, theta, s_mat = mat(0), mat(1), mat(2)
    m = 2.0 * theta - nn(gx, theta, HI)
    m_t = m.T
    cross = nn(m_t, theta, HI)
    gram = s_mat - cross.T - cross + nn(m_t, nn(gx, m, HI), HI)
    fence()
    inv_a = half_inverse(gram[:HALF, :HALF])
    side = nt(gram[HALF:, :HALF], inv_a, HI)
    def gathered():
        fence()
        wait_bytes(b_b2.at[pl.ds(0, NY * NZ - 1)], sems_b[1])
        part = b_b2[0]
        for k in range(1, NY * NZ):
            part = part + b_b2[k]
        b_res[b] = part
        for d in range(1, NCOL):
            send(b_res.at[b], b_res.at[b], coldev(d), sems_b[2])
        fence()

    fence()
    inv_c = half_inverse(gram[HALF:, HALF:] - nt(side, side, HI), gathered)
    corner = nn(inv_c, nn(side, inv_a, HI), HI)
    t_t = jnp.concatenate(
        [jnp.concatenate([inv_a, jnp.zeros((HALF, HALF), F32)], axis=1), jnp.concatenate([-corner, inv_c], axis=1)],
        axis=0)
    fence()
    for h in range(2):
        for d in (1, 3, 2):
            lo_copy[h, d].wait_recv()
    fence()
    mt_t = nt(t_t, m, HI)
    for r in range(4):
        low = [sum(lo_r[h, d, r].astype(F32) for d in range(3)) for h in range(2)]
        lap = lap_ref[r] - jnp.concatenate(low, axis=0)
        part = nn(t_t, lap, HI) - nn(mt_t, xt_ref[r], HI)
        search_ref[r * BS:(r + 1) * BS, :] = part.T.astype(BF16)
    search_copy = pltpu.make_async_copy(search_ref, search_hbm, local_sem.at[3])
    search_copy.start()
    e1 = nt(mt_t, theta, HI)
    e2 = nn(mt_t, s_mat, HI)
    tail = jnp.concatenate([t_t, -mt_t], axis=1)
    proj_ref[0, :BS] = theta
    proj_ref[0, BS:] = nn(t_t, s_mat - cross, HI)
    left_copy = pltpu.make_async_copy(proj_ref.at[0], proj_hbm.at[:, pl.ds(0, BS)], local_sem.at[5])
    left_copy.start()
    fence()
    wait_bytes(b_res.at[pl.ds(0, 7)], sems_b[2])
    fence()
    spun = nn(t_t, b_res[...].reshape(BS, 2 * BS) * inverse, HI)
    xq = spun[:, :BS] - e1
    qq = nt(jnp.concatenate([spun[:, BS:] - e2, xq], axis=1), tail, HI)
    proj_ref[1, :BS] = xq.T
    proj_ref[1, BS:] = qq.T
    proj_copy = pltpu.make_async_copy(proj_ref.at[1], proj_hbm.at[:, pl.ds(BS, BS)], local_sem.at[4])
    proj_copy.start()
    assert counter[0] <= N_SEM
    fence()
    whole = w_ref.at[pl.ds(0, sent[0] // BLOCK_BYTES)]
    assert sent[0] % BLOCK_BYTES == 0
    remote(whole, whole, sibling, 0).wait_send()
    search_copy.wait()
    left_copy.wait()
    proj_copy.wait()


def shards(iterate, blocks, block_row, block_col, block_count):
    shape = jax.ShapeDtypeStruct
    rows1 = HALF + DEG
    node_total = iterate.shape[0] * lax.axis_size("rows") * lax.axis_size("cols")

    def buf(*dims, dtype=F32):
        return pltpu.VMEM(dims, dtype)

    def kernel(*refs):
        step_kernel(1.0 / node_total, *refs)

    outs = (shape(iterate.shape, BF16), shape((2 * BS, 2 * BS), F32))
    hbm = pl.BlockSpec(memory_space=pl.ANY)
    search, projected = pl.pallas_call(
        kernel,
        out_shape=outs,
        in_specs=[hbm, hbm, hbm, hbm, pl.BlockSpec(memory_space=pltpu.SMEM)],
        out_specs=(hbm, hbm),
        scratch_shapes=[
            buf(4 * BS, BS, dtype=BF16), buf(1, SLOTS, dtype=jnp.int32), buf(1, SLOTS, dtype=jnp.int32),
            buf(4 * BS, BS, dtype=BF16), buf(2, 2 * BS, BS),
            buf(SLOTS + 1, BS, BS, dtype=BF16),
            buf(64, HALF, BS, dtype=BF16), buf(64, HALF, BS, dtype=BF16),
            buf(64, HALF, BS, dtype=BF16), buf(64, HALF, BS, dtype=BF16),
            buf(2, PAIRS, rows1, BS), buf(4, BS, BS), buf(8, 512, dtype=jnp.int32), buf(8, 512),
            pltpu.SMEM((8, 512), jnp.int32), pltpu.SMEM((8, 512), F32),
            buf(4, 4, rows1, BS), buf(4, 4, rows1, BS), buf(4, 4, HALF, BS), buf(4, 4, HALF, BS),
            buf(2, 3, 4, HALF, BS, dtype=BF16), buf(2, 3, 4, HALF, BS, dtype=BF16),
            buf(2, 3, 4, HALF, BS, dtype=BF16), buf(2, 3, 4, HALF, BS, dtype=BF16),
            buf(3, 4, DEG, BS), buf(3, 4, DEG, BS),
            buf(4, BS, BS), buf(4, DEG, BS),
            buf(2, 4, 4, BS, BS, dtype=BF16), buf(2, 4, 4, BS, BS, dtype=BF16),
            buf(8, 3, 16, BS), buf(7, 3, 16, BS), buf(4, 3, 16, BS), buf(4, 3, 16, BS), buf(8, 3, 16, BS),
            buf(8, 16, 2 * BS), buf(7, 16, 2 * BS), buf(16, 16, 2 * BS), buf(8, 16, 2 * BS),
            buf(8, BS), pltpu.SemaphoreType.DMA((1,)), pltpu.SemaphoreType.DMA((N_SEM,)), pltpu.SemaphoreType.DMA((10,)),
        ],
        compiler_params=pltpu.CompilerParams(
            collective_id=0, has_side_effects=True, vmem_limit_bytes=60 * 1024 * 1024),
        name="lobpcg_step",
    )(iterate, blocks.reshape(SLOTS, BS, BS), block_row.reshape(1, SLOTS), block_col.reshape(1, SLOTS),
      block_count.reshape(1, 1))

    def hand_over(search_ref, projected_ref, search_out, projected_out, search_v, projected_v, sems):
        pairs = [(search_ref, search_v, search_out)]
        for n in range(2):
            rows = pl.ds(n * BS, BS)
            pairs.append((projected_ref.at[rows], projected_v.at[rows], projected_out.at[rows]))
        reads = [pltpu.make_async_copy(src, mid, sems.at[n]) for n, (src, mid, dst) in enumerate(pairs)]
        writes = [pltpu.make_async_copy(mid, dst, sems.at[n + 3]) for n, (src, mid, dst) in enumerate(pairs)]
        for copy in reads:
            copy.start()
        for n in range(3):
            reads[n].wait()
            writes[n].start()
        for copy in writes:
            copy.wait()

    return pl.pallas_call(
        hand_over, out_shape=outs, in_specs=[hbm, hbm], out_specs=(hbm, hbm),
        scratch_shapes=[buf(4 * BS, BS, dtype=BF16), buf(2 * BS, 2 * BS), pltpu.SemaphoreType.DMA((6,))],
        name="hand_over",
    )(search, projected)


def solution(mesh):
    placed = (
        P(("rows", "cols"), None),
        P("rows", "cols", None, None, None),
        P("rows", "cols", None),
        P("rows", "cols", None),
        P("rows", "cols"),
    )
    return jax.shard_map(
        shards,
        mesh=mesh,
        in_specs=placed,
        out_specs=(P(("rows", "cols"), None), P()),
        check_vma=False,
    )
```
